32 devices in a mesh: cell: 8 (over z, y), gene: 4 (over x, core).
Axes of the slice: x: 2, y: 2, z: 4, core: 2. Of those that a mesh axis runs over, the one named last changes fastest.
Arguments:
- counts: int32 [8192, 16384], P('cell', 'gene'), may hold values from 0 to 4
- factors: float32 [8192, 64], P(('cell', 'gene')), may hold values from -1.5 to 1.5
- loadings: float32 [16384, 64], P(('gene', 'cell')), may hold values from -1.5 to 1.5
- cell_offset: float32 [8192], P('cell'), may hold values from -1.2 to 1.2
- gene_offset: float32 [16384], P('gene'), may hold values from -1.2 to 1.2
Outputs:
- new_factors: float32 [8192, 64], P(('cell', 'gene'))
- new_loadings: float32 [16384, 64], P(('gene', 'cell'))
The draws below stay inside these ranges and needn't reach their ends.
All inputs are finite; a program needn't handle non-finite values.
Results may differ from the reference program's by a relative error of at most 0.0003.
Values sent between devices are 32-bit elements; how exact they have to be, the bound alone decides.
No kernel may reach another device: no remote copies, remote signals or barrier semaphores. Data moves between devices by JAX's collectives and lax.ppermute only.
A program may use at most 128 MiB of HBM per device.

```python
import jax
import jax.numpy as jnp
from jax import lax

K = 64
G = 16384
CELL_DEV = 1024
ITERS = 2
C = 8192
N_CELL = 8


def touch_ends(drawn, rng, low, high):
    dims = drawn.shape
    spot = [jax.random.randint(jax.random.fold_in(rng, axis), (), 0, dims[axis]) for axis in range(len(dims))]
    drawn = drawn.at[tuple(spot)].set(low)
    longest = dims.index(max(dims))
    spot[longest] = (spot[longest] + 1) % dims[longest]
    return drawn.at[tuple(spot)].set(high)


def block_scale(stream_key, extent, shards, low, high):
    factor_of, own = 1.0, jax.random.fold_in(stream_key, 6)
    for axis_at, shards_of in shards:
        heights = jnp.exp(jax.random.uniform(jax.random.fold_in(own, axis_at), (shards_of,), jnp.float32, low / len(shards), high / len(shards)))
        factor_of = factor_of * jnp.repeat(heights, extent[axis_at] // shards_of).reshape([-1 if axis == axis_at else 1 for axis in range(len(extent))])
    return factor_of


def bell_draw(rng, shape, spread, bound, shards=(), held_as=jnp.bfloat16):
    level = block_scale(rng, shape, shards, -0.22, 0.18) if shards else 1.0
    result = jax.random.normal(rng, shape, jnp.float32) * spread * level
    return jnp.minimum(jnp.maximum(result, -bound), bound).astype(held_as)


def setup_inputs(seed: int = 0) -> dict:
    key_list = jax.random.split(jax.random.key(seed), 6)
    counts = touch_ends(jax.random.randint(key_list[0], (C, G), 0, 5), jax.random.fold_in(key_list[0], 1), 0, 4).astype(jnp.int32)
    factors = bell_draw(key_list[1], (C, K), 0.25, 1.5, ((0, 32),), jnp.float32)
    loadings = bell_draw(key_list[2], (G, K), 0.25, 1.5, ((0, 32),), jnp.float32)
    cell_offset = jnp.clip(jax.random.uniform(key_list[3], (C,), jnp.float32, -1.2, 1.2) * block_scale(key_list[3], (C,), ((0, 8),), -0.4, 0.0), -1.2, 1.2)
    gene_offset = jnp.clip(jax.random.uniform(key_list[4], (G,), jnp.float32, -1.2, 1.2) * block_scale(key_list[4], (G,), ((0, 4),), -0.4, 0.0), -1.2, 1.2)
    return dict(counts=counts, factors=factors, loadings=loadings, cell_offset=cell_offset, gene_offset=gene_offset)


epsilon = 1e-6
step_cap = 0.25


def bounded(ratio):
    return step_cap * jnp.tanh(ratio / step_cap)


def predict(factor_rows, loading_rows, cell_part, gene_part, count_part):
    linear = jnp.dot(factor_rows, loading_rows.T, preferred_element_type=jnp.float32, precision=lax.Precision.HIGHEST)
    linear = linear + cell_part[:, None] + gene_part[None, :]
    means = jnp.exp(linear)
    excess = means - count_part.astype(jnp.float32)
    return means, excess


def reference(counts, factors, loadings, cell_offset, gene_offset):
    count_blocks = counts.reshape(N_CELL, CELL_DEV, G)
    offset_blocks = cell_offset.reshape(N_CELL, CELL_DEV)
    current_u = factors
    current_v = loadings
    for iteration in range(ITERS):
        factor_blocks = current_u.reshape(N_CELL, CELL_DEV, K)
        squared_v = current_v * current_v

        def factor_step(items):
            count_part, factor_rows, cell_part = items
            means, excess = predict(factor_rows, current_v, cell_part, gene_offset, count_part)
            grad_u = jnp.dot(excess, current_v, preferred_element_type=jnp.float32, precision=lax.Precision.HIGHEST)
            curv_u = jnp.dot(means, squared_v, preferred_element_type=jnp.float32, precision=lax.Precision.HIGHEST)
            return factor_rows - bounded(grad_u / (curv_u + epsilon))

        new_blocks = lax.map(factor_step, (count_blocks, factor_blocks, offset_blocks))
        current_u = new_blocks.reshape(C, K)

        def loading_sum(carry, items):
            count_part, factor_rows, cell_part = items
            means, excess = predict(factor_rows, current_v, cell_part, gene_offset, count_part)
            grad_v = jnp.dot(excess.T, factor_rows, preferred_element_type=jnp.float32, precision=lax.Precision.HIGHEST)
            curv_v = jnp.dot(means.T, factor_rows * factor_rows, preferred_element_type=jnp.float32, precision=lax.Precision.HIGHEST)
            return (carry[0] + grad_v, carry[1] + curv_v), None

        start = (jnp.zeros((G, K), jnp.float32), jnp.zeros((G, K), jnp.float32))
        totals, unused = lax.scan(loading_sum, start, (count_blocks, new_blocks, offset_blocks))
        current_v = current_v - bounded(totals[0] / (totals[1] + epsilon))
    return current_u, current_v
```

```python
import functools

import jax
import jax.numpy as jnp
from jax import lax
from jax.experimental import pallas as pl
from jax.experimental.pallas import tpu as pltpu
from jax.sharding import PartitionSpec as P

ITERS = 2
LOG2E = 1.4426950408889634
BF = jnp.bfloat16
F32 = jnp.float32
NT = (((1,), (1,)), ((), ()))

epsilon = 1e-06
step_cap = 0.25


def bounded(ratio):
    return step_cap * jnp.tanh(ratio / step_cap)


def params(megabytes=56):
    return pltpu.CompilerParams(vmem_limit_bytes=megabytes * 2**20)


def pack(rows):
    half = rows.shape[0] // 2
    return jnp.concatenate([rows[:half], rows[half:]], axis=1)


def left_lanes(shape):
    return lax.broadcasted_iota(jnp.int32, shape, 1) < 64


def doubled(packed):
    turned = pltpu.roll(packed, 64, 1)
    left = left_lanes(packed.shape)
    return jnp.concatenate(
        [jnp.where(left, packed, turned), jnp.where(left, turned, packed)], axis=0
    )


def parts(x):
    hi = x.astype(BF).astype(F32)
    return hi, x - hi


def pick(left, a, b):
    return jnp.where(left, a, b).astype(BF)


def queries(x, offset):
    left = left_lanes(x.shape)
    hi, lo = parts(x * LOG2E)
    return jnp.concatenate([pick(left, hi, lo), pick(left, hi, offset.astype(F32))], axis=1)


def keys(x, offset):
    left = left_lanes(x.shape)
    hi, lo = parts(x)
    return jnp.concatenate([hi.astype(BF), pick(left, lo, offset.astype(F32))], axis=1)


def weights(x):
    left = left_lanes(x.shape)
    hi, lo = parts(x)
    square_hi, square_lo = parts(x * x)
    both = jnp.concatenate([pick(left, hi, square_hi), pick(left, lo, square_lo)], axis=1)
    grad = jnp.concatenate([pick(left, -hi, 0.0), pick(left, -lo, 0.0)], axis=1)
    return both, grad


def sums(query, key, weight, count, count_weight):
    linear = lax.dot_general(query, key, NT, preferred_element_type=F32)
    means = jnp.exp2(linear)
    hi = means.astype(BF)
    lo = (means - hi.astype(F32)).astype(BF)
    total = jnp.dot(
        jnp.concatenate([hi, lo, count], axis=1),
        jnp.concatenate([weight, weight, count_weight], axis=0),
        preferred_element_type=F32,
    )
    return total[:, :128] + total[:, 128:]


def offset_columns(offset, is_cell):
    x = offset * LOG2E
    hi = lax.reduce_precision(x, 8, 7)
    mid = lax.reduce_precision(x - hi, 8, 7)
    low = x - hi - mid
    one = jnp.ones_like(x)
    columns = [hi, mid, low, one, one, one] if is_cell else [one, one, one, hi, mid, low]
    stacked = jnp.stack(columns, axis=1).astype(BF)
    return jnp.pad(stacked, ((0, 0), (64, 58)))


def count_kernel(count_ref, plain_ref, turned_ref):
    x = count_ref[...].astype(F32).astype(BF)
    plain_ref[...] = x
    turned_ref[...] = x.T


def count_call(counts, tile=512):
    cells, genes = counts.shape
    return pl.pallas_call(
        count_kernel,
        grid=(genes // tile,),
        in_specs=[pl.BlockSpec((cells, tile), lambda j: (0, j))],
        out_specs=[
            pl.BlockSpec((cells, tile), lambda j: (0, j)),
            pl.BlockSpec((tile, cells), lambda j: (j, 0)),
        ],
        out_shape=[
            jax.ShapeDtypeStruct((cells, genes), BF),
            jax.ShapeDtypeStruct((genes, cells), BF),
        ],
        compiler_params=params(),
        cost_estimate=pl.CostEstimate(flops=0, bytes_accessed=counts.size * 8, transcendentals=0),
    )(counts)


def work(cells, genes):
    return pl.CostEstimate(
        flops=2 * cells * genes * 256 * 4,
        bytes_accessed=2 * cells * genes,
        transcendentals=cells * genes,
    )


def factor_kernel(rows, where, u_ref, cell_ref, mine_ref, other_ref, gene_ref, count_ref, sum_ref, out_ref):
    y = where[1]
    first = jnp.where(y == 0, mine_ref[...], other_ref[...])
    second = jnp.where(y == 0, other_ref[...], mine_ref[...])
    v = jnp.concatenate([doubled(first), doubled(second)], axis=0)
    key = keys(v, gene_ref[...])
    weight, count_weight = weights(v)
    query = queries(doubled(u_ref[...]), cell_ref[...])
    for at in range(0, query.shape[0], rows):
        span = slice(at, at + rows)
        out_ref[span, :] = sum_ref[span, :] + sums(
            query[span], key, weight, count_ref[span, :], count_weight
        )


def factor_call(where, u, cell_columns, mine, other, gene_columns, counts, total, rows=256):
    cells = counts.shape[0]
    half = mine.shape[0]
    tile = 4 * half
    whole = lambda shape: pl.BlockSpec(shape, lambda j, w: (0, 0))
    return pl.pallas_call(
        functools.partial(factor_kernel, rows),
        grid_spec=pltpu.PrefetchScalarGridSpec(
            num_scalar_prefetch=1,
            grid=(1,),
            in_specs=[
                whole(u.shape),
                whole(cell_columns.shape),
                whole(mine.shape),
                whole(other.shape),
                pl.BlockSpec((tile, 128), lambda j, w: (w[0], 0)),
                pl.BlockSpec((cells, tile), lambda j, w: (0, w[0])),
                whole((cells, 128)),
            ],
            out_specs=whole((cells, 128)),
        ),
        out_shape=jax.ShapeDtypeStruct((cells, 128), F32),
        input_output_aliases={7: 0},
        compiler_params=params(),
        cost_estimate=work(cells, tile),
    )(where, u, cell_columns, mine, other, gene_columns, counts, total)


def loading_kernel(rows, where, u_ref, cell_ref, mine_ref, other_ref, gene_ref, turned_ref, mine_out, other_out):
    y = where[1]
    u = doubled(u_ref[...])
    key = keys(u, cell_ref[...])
    weight, count_weight = weights(u)
    count = mine_ref.shape[0] * 2
    for target, v_ref, place in ((other_out, other_ref, 1 - y), (mine_out, mine_ref, y)):
        base = place * count
        query = queries(doubled(v_ref[...]), gene_ref[pl.ds(pl.multiple_of(base, count), count), :])
        for at in range(0, count, rows):
            target[at : at + rows, :] = sums(
                query[at : at + rows],
                key,
                weight,
                turned_ref[pl.ds(pl.multiple_of(base + at, rows), rows), :],
                count_weight,
            )


def loading_call(where, u, cell_columns, mine, other, gene_columns, turned, rows=256):
    cells = turned.shape[1]
    half = mine.shape[0]
    tile = 4 * half
    whole = lambda shape: pl.BlockSpec(shape, lambda j, w: (0, 0))
    return pl.pallas_call(
        functools.partial(loading_kernel, rows),
        grid_spec=pltpu.PrefetchScalarGridSpec(
            num_scalar_prefetch=1,
            grid=(1,),
            in_specs=[
                whole(u.shape),
                whole(cell_columns.shape),
                whole(mine.shape),
                whole(other.shape),
                pl.BlockSpec((tile, 128), lambda j, w: (w[0], 0)),
                pl.BlockSpec((tile, cells), lambda j, w: (w[0], 0)),
            ],
            out_specs=[whole((2 * half, 128))] * 2,
        ),
        out_shape=[jax.ShapeDtypeStruct((2 * half, 128), F32)] * 2,
        compiler_params=params(),
        cost_estimate=work(cells, tile),
    )(where, u, cell_columns, mine, other, gene_columns, turned)


def stepped(packed, total):
    half = packed.shape[0]
    step = bounded(total[:, :64] / (total[:, 64:] + epsilon))
    return packed - jnp.concatenate([step[:half], step[half:]], axis=1)


def swap(x, axis, size, mask):
    return lax.ppermute(x, axis, [(i, i ^ mask) for i in range(size)])


def overlapped(counts, factors, loadings, cell_offset, gene_offset, n_cell, n_gene):
    cell = lax.axis_index("cell")
    gene = lax.axis_index("gene")
    core, x = gene % 2, gene // 2
    y, z = cell % 2, cell // 2
    n_z = n_cell // 2

    def over_cell(value, mask):
        return swap(value, "cell", n_cell, mask)

    def over_gene(value, mask):
        return swap(value, "gene", n_gene, mask)

    def in_order(place, mine, other, axis):
        return jnp.where(
            place == 0,
            jnp.concatenate([mine, other], axis=axis),
            jnp.concatenate([other, mine], axis=axis),
        )

    def gather_loadings(own):
        mine = [own] + [over_cell(own, 2 * s) for s in range(1, n_z)]
        other = [over_cell(m, 1) for m in mine]
        return mine, other

    own_v = pack(loadings)
    v_mine, v_other = gather_loadings(own_v)
    u_half = in_order(x, factors, over_gene(factors, 2), 1)
    u_block = in_order(core, u_half, over_gene(u_half, 1), 0)
    plain, turned = count_call(counts)
    cell_columns = offset_columns(cell_offset, True)
    gene_columns = offset_columns(gene_offset, False)
    where = [jnp.stack([z ^ s, y]) for s in range(n_z)]
    rows = factors.shape[0]

    for iteration in range(ITERS):
        total = jnp.zeros((cell_offset.shape[0], 128), F32)
        for s in range(n_z):
            total = factor_call(
                where[s], u_block, cell_columns, v_mine[s], v_other[s], gene_columns, plain, total
            )
        split = total.reshape(2, 2, rows, 128)
        keep = lax.dynamic_index_in_dim(split, core, 1, False).reshape(2 * rows, 128)
        send = lax.dynamic_index_in_dim(split, 1 - core, 1, False).reshape(2 * rows, 128)
        keep = keep + over_gene(send, 1)
        keep = keep + over_gene(keep, 2)
        u_half = stepped(u_half, keep)
        u_block = in_order(core, u_half, over_gene(u_half, 1), 0)

        shares = [None] * n_z
        for s in [2, 3, 1, 0]:
            mine, other = loading_call(
                where[s], u_block, cell_columns, v_mine[s], v_other[s], gene_columns, turned
            )
            mine = mine + over_cell(other, 1)
            shares[s] = mine if s == 0 else over_cell(mine, 2 * s)
        total = shares[0] + shares[1] + shares[2] + shares[3]
        own_v = stepped(own_v, total)
        if iteration + 1 < ITERS:
            v_mine, v_other = gather_loadings(own_v)

    new_u = jnp.where(x == 0, u_half[:, :64], u_half[:, 64:])
    new_v = jnp.concatenate([own_v[:, :64], own_v[:, 64:]], axis=0)
    return new_u, new_v


def predict(factor_rows, loading_rows, cell_part, gene_part, count_part):
    linear = jnp.dot(
        factor_rows,
        loading_rows.T,
        preferred_element_type=jnp.float32,
        precision=lax.Precision.HIGHEST,
    )
    linear = linear + cell_part[:, None] + gene_part[None, :]
    means = jnp.exp(linear)
    excess = means - count_part.astype(jnp.float32)
    return (means, excess)


def plain_sweeps(counts, factors, loadings, cell_offset, gene_offset):
    rank = factors.shape[1]
    precise = dict(preferred_element_type=F32, precision=lax.Precision.HIGHEST)
    contract = (((0,), (0,)), ((), ()))
    own_u, own_v = factors, loadings
    u = lax.all_gather(own_u, "gene", axis=0, tiled=True)
    v = lax.all_gather(own_v, "cell", axis=0, tiled=True)
    for iteration in range(ITERS):
        means, excess = predict(u, v, cell_offset, gene_offset, counts)
        grad = jnp.dot(excess, v, **precise)
        curv = jnp.dot(means, v * v, **precise)
        shares = lax.psum_scatter(
            jnp.concatenate([grad, curv], axis=1), "gene", scatter_dimension=0, tiled=True
        )
        own_u = own_u - bounded(shares[:, :rank] / (shares[:, rank:] + epsilon))
        u = lax.all_gather(own_u, "gene", axis=0, tiled=True)
        means, excess = predict(u, v, cell_offset, gene_offset, counts)
        grad = lax.dot_general(excess, u, contract, **precise)
        curv = lax.dot_general(means, u * u, contract, **precise)
        shares = lax.psum_scatter(
            jnp.concatenate([grad, curv], axis=1), "cell", scatter_dimension=0, tiled=True
        )
        own_v = own_v - bounded(shares[:, :rank] / (shares[:, rank:] + epsilon))
        if iteration + 1 < ITERS:
            v = lax.all_gather(own_v, "cell", axis=0, tiled=True)
    return own_u, own_v


def solution(mesh):
    n_cell, n_gene = mesh.shape["cell"], mesh.shape["gene"]
    in_specs = (
        P("cell", "gene"),
        P(("cell", "gene"), None),
        P(("gene", "cell"), None),
        P("cell"),
        P("gene"),
    )
    out_specs = (P(("cell", "gene"), None), P(("gene", "cell"), None))
    per_device = plain_sweeps
    if (n_cell, n_gene) == (8, 4):
        per_device = functools.partial(overlapped, n_cell=n_cell, n_gene=n_gene)
    return jax.shard_map(
        per_device, mesh=mesh, in_specs=in_specs, out_specs=out_specs, check_vma=False
    )
```

```python
import functools

import jax
import jax.numpy as jnp
from jax import lax
from jax.experimental import pallas as pl
from jax.experimental.pallas import tpu as pltpu
from jax.sharding import PartitionSpec as P

ITERS = 2
LOG2E = 1.4426950408889634
BF = jnp.bfloat16
F32 = jnp.float32
NT = (((1,), (1,)), ((), ()))

epsilon = 1e-06
step_cap = 0.25


def bounded(ratio):
    return step_cap * jnp.tanh(ratio / step_cap)


def params(megabytes=14):
    return pltpu.CompilerParams(vmem_limit_bytes=megabytes * 2**20)


def pack(rows):
    half = rows.shape[0] // 2
    return jnp.concatenate([rows[:half], rows[half:]], axis=1)


def left_lanes(shape):
    return lax.broadcasted_iota(jnp.int32, shape, 1) < 64


def doubled(packed):
    turned = pltpu.roll(packed, 64, 1)
    left = left_lanes(packed.shape)
    return jnp.concatenate(
        [jnp.where(left, packed, turned), jnp.where(left, turned, packed)], axis=0
    )


def parts(x):
    hi = x.astype(BF).astype(F32)
    return hi, x - hi


def pick(left, a, b):
    return jnp.where(left, a, b).astype(BF)


def queries(x, offset):
    left = left_lanes(x.shape)
    hi, lo = parts(x * LOG2E)
    return jnp.concatenate([pick(left, hi, lo), pick(left, hi, offset.astype(F32))], axis=1)


def keys(x, offset):
    left = left_lanes(x.shape)
    hi, lo = parts(x)
    return jnp.concatenate([hi.astype(BF), pick(left, lo, offset.astype(F32))], axis=1)


def weights(x):
    left = left_lanes(x.shape)
    hi, lo = parts(x)
    square_hi, square_lo = parts(x * x)
    both = jnp.concatenate([pick(left, hi, square_hi), pick(left, lo, square_lo)], axis=1)
    grad = jnp.concatenate([pick(left, -hi, 0.0), pick(left, -lo, 0.0)], axis=1)
    return both, grad


def sums(query, key, weight, count, count_weight):
    linear = lax.dot_general(query, key, NT, preferred_element_type=F32)
    means = jnp.exp2(linear)
    hi = means.astype(BF)
    lo = (means - hi.astype(F32)).astype(BF)
    total = jnp.dot(
        jnp.concatenate([hi, lo, count], axis=1),
        jnp.concatenate([weight, weight, count_weight], axis=0),
        preferred_element_type=F32,
    )
    return total[:, :128] + total[:, 128:]


def columns_kernel(is_cell, offset_ref, out_ref):
    hi, rest = parts(offset_ref[...] * LOG2E)
    mid, low = parts(rest)
    shape = (128, offset_ref.shape[1])
    row = lax.broadcasted_iota(jnp.int32, shape, 0)
    first, ones = (64, 67) if is_cell else (67, 64)
    lines = jnp.where((row >= ones) & (row < ones + 3), 1.0, 0.0)
    for at, part in enumerate((hi, mid, low)):
        lines = jnp.where(row == first + at, part, lines)
    out_ref[...] = lines.T.astype(BF)


def columns_call(offset, is_cell):
    size = offset.shape[0]
    return pl.pallas_call(
        functools.partial(columns_kernel, is_cell),
        out_shape=jax.ShapeDtypeStruct((size, 128), BF),
        compiler_params=params(),
        cost_estimate=work(0, 0),
    )(offset.reshape(1, size))


def count_kernel(tile, where, count_ref, plain_ref, turned_ref):
    at = pl.ds(pl.multiple_of(pl.program_id(0) * tile, tile), tile)
    x = count_ref[...].astype(F32).astype(BF)
    plain_ref[:, at] = x
    turned_ref[at, :] = x.T


def count_call(where, counts, blocks=2, tile=512):
    cells, genes = counts.shape
    genes = genes // blocks
    steps = genes // tile
    return pl.pallas_call(
        functools.partial(count_kernel, tile),
        grid_spec=pltpu.PrefetchScalarGridSpec(
            num_scalar_prefetch=1,
            grid=(steps,),
            in_specs=[pl.BlockSpec((cells, tile), lambda j, w: (0, w[0] * steps + j))],
            out_specs=[pl.BlockSpec(memory_space=pltpu.VMEM)] * 2,
        ),
        out_shape=[
            jax.ShapeDtypeStruct((cells, genes), BF),
            jax.ShapeDtypeStruct((genes, cells), BF),
        ],
        compiler_params=params(42),
        cost_estimate=pl.CostEstimate(flops=0, bytes_accessed=cells * genes * 6, transcendentals=0),
    )(where, counts)


def work(cells, genes):
    return pl.CostEstimate(
        flops=2 * cells * genes * 256 * 4,
        bytes_accessed=2 * cells * genes,
        transcendentals=cells * genes,
    )


def factor_rows(core, mine_ref, other_ref):
    mine, other = mine_ref[...], other_ref[...]
    first = jnp.where(core == 0, mine, other)
    second = jnp.where(core == 0, other, mine)
    return doubled(jnp.concatenate([first, second], axis=0))


def chunk_base(where, slot, place, size):
    at = (jnp.bitwise_xor(where[1], slot) * 2 + place) * size
    return pl.multiple_of(at, size)


def factor_kernel(last, where, mine_u, other_u, cell_ref, v0, w0, v1, w1, gene_ref, count_ref, turned_ref, *rest):
    y, core = where[2], where[3]
    if last:
        sum_ref, keep_ref, send_ref, query_ref = rest
    else:
        out_ref, query_ref = rest
    query_ref[...] = queries(factor_rows(core, mine_u, other_u), cell_ref[...])
    size = v0.shape[0] * 2
    chunks = []
    for slot, refs in enumerate(((v0, w0), (v1, w1))):
        for place, ref in zip((y, 1 - y), refs):
            base = chunk_base(where, slot, place, size)
            v = doubled(ref[...])
            at = pl.ds(base, size)
            chunks.append((at, keys(v, gene_ref[at, :]), *weights(v)))
    rows = mine_u.shape[0]

    def partial_sums(row):
        span = pl.ds(row, rows)
        query = query_ref[span, :]
        total = sum_ref[span, :] if last else None
        for at, key, weight, count_weight in chunks:
            part = sums(query, key, weight, count_ref[span, at], count_weight)
            total = part if total is None else total + part
        return total

    for side in range(2):
        if last:
            for target, place in ((send_ref, 1 - core), (keep_ref, core)):
                row = pl.multiple_of(side * 2 * rows + place * rows, rows)
                target[side * rows : (side + 1) * rows, :] = partial_sums(row)
        else:
            for row in (side * 2 * rows, side * 2 * rows + rows):
                out_ref[row : row + rows, :] = partial_sums(row)


def block_specs(arrays):
    return [pl.BlockSpec(a.shape, lambda j, w: (0, 0)) for a in arrays]


def factor_call(where, u, cell_columns, v, gene_columns, counts, total=None):
    cells = counts[0].shape[0]
    tile = 8 * v[0].shape[0]
    last = total is not None
    whole = [*u, cell_columns, *v]
    extra = [total] if last else []
    shapes = [(cells // 2, 128)] * 2 if last else [(cells, 128)]
    return pl.pallas_call(
        functools.partial(factor_kernel, last),
        grid_spec=pltpu.PrefetchScalarGridSpec(
            num_scalar_prefetch=1,
            grid=(1,),
            in_specs=block_specs(whole)
            + [
                pl.BlockSpec((tile, 128), lambda j, w: (w[0], 0)),
                pl.BlockSpec(memory_space=pltpu.VMEM),
                pl.BlockSpec(memory_space=pl.ANY),
            ]
            + block_specs(extra),
            out_specs=[pl.BlockSpec(shape, lambda j, w: (0, 0)) for shape in shapes],
            scratch_shapes=[pltpu.VMEM((cells, 256), BF)],
        ),
        out_shape=[jax.ShapeDtypeStruct(shape, F32) for shape in shapes],
        compiler_params=params(),
        cost_estimate=work(cells, tile),
    )(where, *whole, gene_columns, *counts, *extra)


def loading_kernel(pieces, slots, where, mine_u, other_u, cell_ref, *rest):
    y, core = where[2], where[3]
    v, (gene_ref, turned_ref), outs = rest[: 2 * slots], rest[2 * slots :][:2], iter(rest[2 * slots + 2 :])
    u = factor_rows(core, mine_u, other_u)
    key = keys(u, cell_ref[...])
    weight, count_weight = weights(u)
    size = v[0].shape[0] * 2
    rows = size // 2
    for slot in reversed(range(slots)):
        for place, ref in ((1 - y, v[2 * slot + 1]), (y, v[2 * slot])):
            base = chunk_base(where, slot, place, size)
            query = queries(doubled(ref[...]), gene_ref[pl.ds(base, size), :])
            for half in range(2):
                if half == 0 or pieces == 2:
                    target = next(outs)
                row = half * rows if pieces == 1 else 0
                count = turned_ref[pl.ds(pl.multiple_of(base + half * rows, rows), rows), :]
                span = slice(half * rows, (half + 1) * rows)
                target[row : row + rows, :] = sums(query[span], key, weight, count, count_weight)


def loading_call(where, u, cell_columns, v, gene_columns, turned, pieces):
    cells = turned.shape[1]
    slots = len(v) // 2
    tile = 4 * slots * v[0].shape[0]
    whole = [*u, cell_columns, *v]
    shape = (2 * v[0].shape[0] // pieces, 128)
    return pl.pallas_call(
        functools.partial(loading_kernel, pieces, slots),
        grid_spec=pltpu.PrefetchScalarGridSpec(
            num_scalar_prefetch=1,
            grid=(1,),
            in_specs=block_specs(whole)
            + [
                pl.BlockSpec((tile, 128), lambda j, w: (w[0], 0)),
                pl.BlockSpec(memory_space=pltpu.VMEM),
            ],
            out_specs=[pl.BlockSpec(shape, lambda j, w: (0, 0))] * (2 * slots * pieces),
        ),
        out_shape=[jax.ShapeDtypeStruct(shape, F32)] * (2 * slots * pieces),
        compiler_params=params(),
        cost_estimate=work(cells, tile),
    )(where, *whole, gene_columns, turned)


def stepped(packed, total):
    half = packed.shape[0]
    step = bounded(total[:, :64] / (total[:, 64:] + epsilon))
    return packed - jnp.concatenate([step[:half], step[half:]], axis=1)


def swap(x, axis, size, mask):
    return lax.ppermute(x, axis, [(i, i ^ mask) for i in range(size)])


def after(value, *others):
    return lax.optimization_barrier((value, *others))[0]


def overlapped(counts, factors, loadings, cell_offset, gene_offset, n_cell, n_gene):
    cell = lax.axis_index("cell")
    gene = lax.axis_index("gene")
    core, x = gene % 2, gene // 2
    y, z = cell % 2, cell // 2

    def over_cell(value, mask):
        return swap(value, "cell", n_cell, mask)

    def over_gene(value, mask):
        return swap(value, "gene", n_gene, mask)

    def gather_loadings(own):
        mine = [own] + [over_cell(own, 2 * s) for s in range(1, 4)]
        other = [over_cell(m, 1) for m in mine]
        return (mine[0], other[0], mine[1], other[1]), (mine[2], other[2], mine[3], other[3])

    own_v = pack(loadings)
    theirs = over_gene(factors, 2)
    own_u = jnp.where(
        x == 0,
        jnp.concatenate([factors, theirs], axis=1),
        jnp.concatenate([theirs, factors], axis=1),
    )
    u = (own_u, over_gene(own_u, 1))
    near, far = gather_loadings(own_v)
    cell_columns = columns_call(cell_offset, True)
    gene_columns = columns_call(gene_offset, False)
    near_at = jnp.stack([z // 2, z % 2, y, core])
    far_at = jnp.stack([(z // 2) ^ 1, z % 2, y, core])
    near_counts = far_counts = None

    for iteration in range(ITERS):
        if iteration == 0:
            near_counts = count_call(near_at, counts)
        (total,) = factor_call(near_at, u, cell_columns, near, gene_columns, near_counts)
        if iteration == 0:
            far_counts = count_call(after(far_at, total), counts)
        keep, send = factor_call(far_at, u, cell_columns, far, gene_columns, far_counts, total)
        keep = keep + over_gene(send, 1)
        keep = keep + over_gene(keep, 2)
        own_u = stepped(own_u, keep)
        u = (own_u, over_gene(own_u, 1))

        o3a, o3b, m3a, m3b, o2a, o2b, m2a, m2b = loading_call(
            far_at, u, cell_columns, far, gene_columns, far_counts[1], 2
        )
        o3a, o3b, o2a, o2b = [over_cell(o, 1) for o in (o3a, o3b, o2a, o2b)]
        m3a = m3a + o3a
        o1, m1, o0, m0 = loading_call(
            after(near_at, m3a), u, cell_columns, near, gene_columns, near_counts[1], 1
        )
        o1, o0 = over_cell(o1, 1), over_cell(o0, 1)
        m3a, m3b = over_cell(m3a, 2), over_cell(m3b + o3b, 2)
        m2a, m2b = over_cell(m2a + o2a + m3a, 4), over_cell(m2b + o2b + m3b, 4)
        m1 = over_cell(m1 + o1, 2)
        own_v = stepped(own_v, m0 + o0 + m1 + jnp.concatenate([m2a, m2b], axis=0))
        if iteration + 1 < ITERS:
            near, far = gather_loadings(own_v)

    new_u = jnp.where(x == 0, own_u[:, :64], own_u[:, 64:])
    new_v = jnp.concatenate([own_v[:, :64], own_v[:, 64:]], axis=0)
    return new_u, new_v


def predict(factor_rows, loading_rows, cell_part, gene_part, count_part):
    linear = jnp.dot(
        factor_rows,
        loading_rows.T,
        preferred_element_type=jnp.float32,
        precision=lax.Precision.HIGHEST,
    )
    linear = linear + cell_part[:, None] + gene_part[None, :]
    means = jnp.exp(linear)
    excess = means - count_part.astype(jnp.float32)
    return (means, excess)


def plain_sweeps(counts, factors, loadings, cell_offset, gene_offset):
    rank = factors.shape[1]
    precise = dict(preferred_element_type=F32, precision=lax.Precision.HIGHEST)
    contract = (((0,), (0,)), ((), ()))
    own_u, own_v = factors, loadings
    u = lax.all_gather(own_u, "gene", axis=0, tiled=True)
    v = lax.all_gather(own_v, "cell", axis=0, tiled=True)
    for iteration in range(ITERS):
        means, excess = predict(u, v, cell_offset, gene_offset, counts)
        grad = jnp.dot(excess, v, **precise)
        curv = jnp.dot(means, v * v, **precise)
        shares = lax.psum_scatter(
            jnp.concatenate([grad, curv], axis=1), "gene", scatter_dimension=0, tiled=True
        )
        own_u = own_u - bounded(shares[:, :rank] / (shares[:, rank:] + epsilon))
        u = lax.all_gather(own_u, "gene", axis=0, tiled=True)
        means, excess = predict(u, v, cell_offset, gene_offset, counts)
        grad = lax.dot_general(excess, u, contract, **precise)
        curv = lax.dot_general(means, u * u, contract, **precise)
        shares = lax.psum_scatter(
            jnp.concatenate([grad, curv], axis=1), "cell", scatter_dimension=0, tiled=True
        )
        own_v = own_v - bounded(shares[:, :rank] / (shares[:, rank:] + epsilon))
        if iteration + 1 < ITERS:
            v = lax.all_gather(own_v, "cell", axis=0, tiled=True)
    return own_u, own_v


def solution(mesh):
    n_cell, n_gene = mesh.shape["cell"], mesh.shape["gene"]
    in_specs = (
        P("cell", "gene"),
        P(("cell", "gene"), None),
        P(("gene", "cell"), None),
        P("cell"),
        P("gene"),
    )
    out_specs = (P(("cell", "gene"), None), P(("gene", "cell"), None))
    per_device = plain_sweeps
    if (n_cell, n_gene) == (8, 4):
        per_device = functools.partial(overlapped, n_cell=n_cell, n_gene=n_gene)
    return jax.shard_map(
        per_device, mesh=mesh, in_specs=in_specs, out_specs=out_specs, check_vma=False
    )
```

```python
import functools

import jax
import jax.numpy as jnp
from jax import lax
from jax.experimental import pallas as pl
from jax.experimental.pallas import tpu as pltpu
from jax.sharding import PartitionSpec as P

ITERS = 2
LOG2E = 1.4426950408889634
BF = jnp.bfloat16
F32 = jnp.float32
NT = (((1,), (1,)), ((), ()))

epsilon = 1e-06
step_cap = 0.25


def bounded(ratio):
    return step_cap * jnp.tanh(ratio / step_cap)


def params(megabytes=14):
    return pltpu.CompilerParams(vmem_limit_bytes=megabytes * 2**20)


def pack(rows):
    half = rows.shape[0] // 2
    return jnp.concatenate([rows[:half], rows[half:]], axis=1)


def left_lanes(shape):
    return lax.broadcasted_iota(jnp.int32, shape, 1) < 64


def doubled(packed):
    turned = pltpu.roll(packed, 64, 1)
    left = left_lanes(packed.shape)
    return jnp.concatenate(
        [jnp.where(left, packed, turned), jnp.where(left, turned, packed)], axis=0
    )


def parts(x):
    hi = x.astype(BF).astype(F32)
    return hi, x - hi


def pick(left, a, b):
    return jnp.where(left, a, b).astype(BF)


def queries(x, offset):
    left = left_lanes(x.shape)
    hi, lo = parts(x * LOG2E)
    return jnp.concatenate([pick(left, hi, lo), pick(left, hi, offset.astype(F32))], axis=1)


def keys(x, offset):
    left = left_lanes(x.shape)
    hi, lo = parts(x)
    return jnp.concatenate([hi.astype(BF), pick(left, lo, offset.astype(F32))], axis=1)


def weights(x):
    left = left_lanes(x.shape)
    hi, lo = parts(x)
    square_hi, square_lo = parts(x * x)
    both = jnp.concatenate([pick(left, hi, square_hi), pick(left, lo, square_lo)], axis=1)
    grad = jnp.concatenate([pick(left, -hi, 0.0), pick(left, -lo, 0.0)], axis=1)
    return both, grad


def sums(query, key, weight, count, count_weight):
    linear = lax.dot_general(query, key, NT, preferred_element_type=F32)
    means = jnp.exp2(linear)
    hi = means.astype(BF)
    lo = (means - hi.astype(F32)).astype(BF)
    total = jnp.dot(
        jnp.concatenate([hi, lo, count], axis=1),
        jnp.concatenate([weight, weight, count_weight], axis=0),
        preferred_element_type=F32,
    )
    return total[:, :128] + total[:, 128:]


def columns_kernel(is_cell, offset_ref, out_ref):
    hi, rest = parts(offset_ref[...] * LOG2E)
    mid, low = parts(rest)
    shape = (128, offset_ref.shape[1])
    row = lax.broadcasted_iota(jnp.int32, shape, 0)
    first, ones = (64, 67) if is_cell else (67, 64)
    lines = jnp.where((row >= ones) & (row < ones + 3), 1.0, 0.0)
    for at, part in enumerate((hi, mid, low)):
        lines = jnp.where(row == first + at, part, lines)
    out_ref[...] = lines.T.astype(BF)


def columns_call(offset, is_cell):
    size = offset.shape[0]
    return pl.pallas_call(
        functools.partial(columns_kernel, is_cell),
        out_shape=jax.ShapeDtypeStruct((size, 128), BF),
        compiler_params=params(),
        cost_estimate=work(0, 0),
    )(offset.reshape(1, size))


def count_kernel(tile, where, count_ref, plain_ref, turned_ref):
    at = pl.ds(pl.multiple_of(pl.program_id(0) * tile, tile), tile)
    x = count_ref[...].astype(F32).astype(BF)
    plain_ref[:, at] = x
    turned_ref[at, :] = x.T


def count_call(where, counts, blocks=2, tile=512):
    cells, genes = counts.shape
    genes = genes // blocks
    steps = genes // tile
    return pl.pallas_call(
        functools.partial(count_kernel, tile),
        grid_spec=pltpu.PrefetchScalarGridSpec(
            num_scalar_prefetch=1,
            grid=(steps,),
            in_specs=[pl.BlockSpec((cells, tile), lambda j, w: (0, w[0] * steps + j))],
            out_specs=[pl.BlockSpec(memory_space=pltpu.VMEM)] * 2,
        ),
        out_shape=[
            jax.ShapeDtypeStruct((cells, genes), BF),
            jax.ShapeDtypeStruct((genes, cells), BF),
        ],
        compiler_params=params(42),
        cost_estimate=pl.CostEstimate(flops=0, bytes_accessed=cells * genes * 6, transcendentals=0),
    )(where, counts)


def work(cells, genes):
    return pl.CostEstimate(
        flops=2 * cells * genes * 256 * 4,
        bytes_accessed=2 * cells * genes,
        transcendentals=cells * genes,
    )


def factor_rows(core, mine_ref, other_ref):
    mine, other = mine_ref[...], other_ref[...]
    first = jnp.where(core == 0, mine, other)
    second = jnp.where(core == 0, other, mine)
    return doubled(jnp.concatenate([first, second], axis=0))


def chunk_base(where, slot, place, size):
    at = (jnp.bitwise_xor(where[1], slot) * 2 + place) * size
    return pl.multiple_of(at, size)


def factor_kernel(mode, where, mine_u, other_u, cell_ref, v0, w0, v1, w1, gene_ref, count_ref, turned_ref, *rest):
    y, core = where[2], where[3]
    if mode == "last":
        sum_ref, keep_ref, send_ref, query_ref = rest
    elif mode == "fresh":
        raw_ref, out_ref, plain_out, turned_out, query_ref, loaded, sem = rest
    else:
        out_ref, query_ref = rest
    size = v0.shape[0] * 2
    copies = []
    if mode == "fresh":
        for at in range(4):
            far = jnp.bitwise_xor(where[0], 1) * 4 + at
            columns = pl.ds(pl.multiple_of(far * size, size), size)
            copies.append(pltpu.make_async_copy(raw_ref.at[:, columns], loaded.at[at], sem.at[at]))
            copies[-1].start()
    query_ref[...] = queries(factor_rows(core, mine_u, other_u), cell_ref[...])
    chunks = []
    for slot, refs in enumerate(((v0, w0), (v1, w1))):
        for place, ref in zip((y, 1 - y), refs):
            base = chunk_base(where, slot, place, size)
            v = doubled(ref[...])
            at = pl.ds(base, size)
            columns = gene_ref[pl.ds(pl.multiple_of(where[0] * 4 * size + base, size), size), :]
            chunks.append((at, keys(v, columns), *weights(v)))
    rows = mine_u.shape[0]

    def partial_sums(row):
        span = pl.ds(row, rows)
        query = query_ref[span, :]
        total = sum_ref[span, :] if mode == "last" else None
        for at, key, weight, count_weight in chunks:
            part = sums(query, key, weight, count_ref[span, at], count_weight)
            total = part if total is None else total + part
        return total

    for step in range(4):
        side = step // 2
        if mode == "last":
            target, place = ((send_ref, 1 - core), (keep_ref, core))[step % 2]
            row = pl.multiple_of(side * 2 * rows + place * rows, rows)
            target[side * rows : (side + 1) * rows, :] = partial_sums(row)
        else:
            out_ref[step * rows : (step + 1) * rows, :] = partial_sums(step * rows)
        if copies:
            columns = slice(step * size, (step + 1) * size)
            copies[step].wait()
            x = loaded[step].astype(F32).astype(BF)
            plain_out[:, columns] = x
            turned_out[columns, :] = x.T


def in_vmem(count):
    return [pl.BlockSpec(memory_space=pltpu.VMEM)] * count


def factor_call(where, u, cell_columns, v, gene_columns, counts, total=None, raw=None):
    cells = counts[0].shape[0]
    size = 2 * v[0].shape[0]
    tile = 4 * size
    mode = "first" if total is None else "last"
    extra, scratch = [], [pltpu.VMEM((cells, 256), BF)]
    shapes = [(cells, 128)]
    if total is not None:
        extra, shapes = [total], [(cells // 2, 128)] * 2
    out_shape = [jax.ShapeDtypeStruct(shape, F32) for shape in shapes]
    extra_specs = in_vmem(len(extra))
    if raw is not None:
        mode = "fresh"
        extra, extra_specs = [raw], [pl.BlockSpec(memory_space=pl.ANY)]
        out_shape += [jax.ShapeDtypeStruct((cells, tile), BF), jax.ShapeDtypeStruct((tile, cells), BF)]
        scratch += [pltpu.VMEM((4, cells, size), raw.dtype), pltpu.SemaphoreType.DMA((4,))]
    operands = [*u, cell_columns, *v, gene_columns, counts[0]]
    return pl.pallas_call(
        functools.partial(factor_kernel, mode),
        in_specs=[pl.BlockSpec(memory_space=pltpu.SMEM)]
        + in_vmem(len(operands))
        + [pl.BlockSpec(memory_space=pl.ANY)]
        + extra_specs,
        out_specs=in_vmem(len(out_shape)),
        out_shape=out_shape,
        scratch_shapes=scratch,
        compiler_params=params(34) if raw is not None else params(),
        cost_estimate=work(cells, tile),
    )(where, *operands, counts[1], *extra)


def loading_kernel(pieces, slots, where, mine_u, other_u, cell_ref, *rest):
    y, core = where[2], where[3]
    count = 2 * len(slots)
    v, (gene_ref, turned_ref), outs = rest[:count], rest[count:][:2], iter(rest[count + 2 :])
    u = factor_rows(core, mine_u, other_u)
    key = keys(u, cell_ref[...])
    weight, count_weight = weights(u)
    size = v[0].shape[0] * 2
    rows = size // 2
    for i, slot in enumerate(slots):
        halves = pieces[i] == 2
        for place, ref in ((1 - y, v[2 * i + 1]), (y, v[2 * i])):
            base = chunk_base(where, slot, place, size)
            columns = gene_ref[pl.ds(pl.multiple_of(where[0] * 4 * size + base, size), size), :]
            query = queries(doubled(ref[...]), columns)
            for half in range(2):
                if half == 0 or halves:
                    target = next(outs)
                row = 0 if halves else half * rows
                part = turned_ref[pl.ds(pl.multiple_of(base + half * rows, rows), rows), :]
                span = slice(half * rows, (half + 1) * rows)
                target[row : row + rows, :] = sums(query[span], key, weight, part, count_weight)


def loading_call(where, u, cell_columns, v, slots, gene_columns, turned, pieces):
    cells = turned.shape[1]
    half = v[0].shape[0]
    v = [part for slot in slots for part in v[2 * slot : 2 * slot + 2]]
    shapes = [(2 * half // count, 128) for count in pieces for _ in range(2 * count)]
    operands = [*u, cell_columns, *v, gene_columns, turned]
    return pl.pallas_call(
        functools.partial(loading_kernel, pieces, slots),
        in_specs=[pl.BlockSpec(memory_space=pltpu.SMEM)] + in_vmem(len(operands)),
        out_specs=in_vmem(len(shapes)),
        out_shape=[jax.ShapeDtypeStruct(shape, F32) for shape in shapes],
        compiler_params=params(),
        cost_estimate=work(cells, 4 * half * len(slots)),
    )(where, *operands)


def stepped(packed, total):
    half = packed.shape[0]
    step = bounded(total[:, :64] / (total[:, 64:] + epsilon))
    return packed - jnp.concatenate([step[:half], step[half:]], axis=1)


def swap(x, axis, size, mask):
    return lax.ppermute(x, axis, [(i, i ^ mask) for i in range(size)])


def after(value, *others):
    return lax.optimization_barrier((value, *others))[0]


def overlapped(counts, factors, loadings, cell_offset, gene_offset, n_cell, n_gene):
    cell = lax.axis_index("cell")
    gene = lax.axis_index("gene")
    core, x = gene % 2, gene // 2
    y, z = cell % 2, cell // 2

    def over_cell(value, mask):
        return swap(value, "cell", n_cell, mask)

    def over_gene(value, mask):
        return swap(value, "gene", n_gene, mask)

    def gather_loadings(own):
        mine = [own] + [over_cell(own, 2 * s) for s in range(1, 4)]
        other = [over_cell(m, 1) for m in mine]
        return (mine[0], other[0], mine[1], other[1]), (mine[2], other[2], mine[3], other[3])

    own_v = pack(loadings)
    theirs = over_gene(factors, 2)
    own_u = jnp.where(
        x == 0,
        jnp.concatenate([factors, theirs], axis=1),
        jnp.concatenate([theirs, factors], axis=1),
    )
    u = (own_u, over_gene(own_u, 1))
    near, far = gather_loadings(own_v)
    cell_columns = columns_call(cell_offset, True)
    gene_columns = columns_call(gene_offset, False)
    near_at = jnp.stack([z // 2, z % 2, y, core])
    far_at = jnp.stack([(z // 2) ^ 1, z % 2, y, core])
    near_counts = count_call(near_at, counts)
    far_counts = None

    for iteration in range(ITERS):
        if far_counts is None:
            total, *far_counts = factor_call(
                near_at, u, cell_columns, near, gene_columns, near_counts, raw=counts
            )
        else:
            (total,) = factor_call(near_at, u, cell_columns, near, gene_columns, near_counts)
        keep, send = factor_call(far_at, u, cell_columns, far, gene_columns, far_counts, total)
        keep = keep + over_gene(send, 1)
        keep = keep + over_gene(keep, 2)
        own_u = stepped(own_u, keep)
        u = (own_u, over_gene(own_u, 1))

        def sums_of(at, v, slots, block, pieces):
            return loading_call(at, u, cell_columns, v, slots, gene_columns, block[1], pieces)

        o3a, o3b, m3a, m3b, o2a, o2b, m2a, m2b = sums_of(far_at, far, (1, 0), far_counts, (2, 2))
        o3a, o3b, o2a, o2b = [over_cell(o, 1) for o in (o3a, o3b, o2a, o2b)]
        m3a, m3b = m3a + o3a, m3b + o3b
        o1, m1 = sums_of(after(near_at, m3a), near, (1,), near_counts, (1,))
        o1 = over_cell(o1, 1)
        m3a, m3b = over_cell(m3a, 2), over_cell(m3b, 2)
        m2a = m2a + o2a + m3a
        o0, m0 = sums_of(after(near_at, m2a, m1), near, (0,), near_counts, (1,))
        m2a, m2b = over_cell(m2a, 4), over_cell(m2b + o2b + m3b, 4)
        m1 = over_cell(m1 + o1, 2)
        m0 = m0 + over_cell(o0, 1)
        own_v = stepped(own_v, m0 + m1 + jnp.concatenate([m2a, m2b], axis=0))
        if iteration + 1 < ITERS:
            near, far = gather_loadings(own_v)

    new_u = jnp.where(x == 0, own_u[:, :64], own_u[:, 64:])
    new_v = jnp.concatenate([own_v[:, :64], own_v[:, 64:]], axis=0)
    return new_u, new_v


def predict(factor_rows, loading_rows, cell_part, gene_part, count_part):
    linear = jnp.dot(
        factor_rows,
        loading_rows.T,
        preferred_element_type=jnp.float32,
        precision=lax.Precision.HIGHEST,
    )
    linear = linear + cell_part[:, None] + gene_part[None, :]
    means = jnp.exp(linear)
    excess = means - count_part.astype(jnp.float32)
    return (means, excess)


def plain_sweeps(counts, factors, loadings, cell_offset, gene_offset):
    rank = factors.shape[1]
    precise = dict(preferred_element_type=F32, precision=lax.Precision.HIGHEST)
    contract = (((0,), (0,)), ((), ()))
    own_u, own_v = factors, loadings
    u = lax.all_gather(own_u, "gene", axis=0, tiled=True)
    v = lax.all_gather(own_v, "cell", axis=0, tiled=True)
    for iteration in range(ITERS):
        means, excess = predict(u, v, cell_offset, gene_offset, counts)
        grad = jnp.dot(excess, v, **precise)
        curv = jnp.dot(means, v * v, **precise)
        shares = lax.psum_scatter(
            jnp.concatenate([grad, curv], axis=1), "gene", scatter_dimension=0, tiled=True
        )
        own_u = own_u - bounded(shares[:, :rank] / (shares[:, rank:] + epsilon))
        u = lax.all_gather(own_u, "gene", axis=0, tiled=True)
        means, excess = predict(u, v, cell_offset, gene_offset, counts)
        grad = lax.dot_general(excess, u, contract, **precise)
        curv = lax.dot_general(means, u * u, contract, **precise)
        shares = lax.psum_scatter(
            jnp.concatenate([grad, curv], axis=1), "cell", scatter_dimension=0, tiled=True
        )
        own_v = own_v - bounded(shares[:, :rank] / (shares[:, rank:] + epsilon))
        if iteration + 1 < ITERS:
            v = lax.all_gather(own_v, "cell", axis=0, tiled=True)
    return own_u, own_v


def solution(mesh):
    n_cell, n_gene = mesh.shape["cell"], mesh.shape["gene"]
    in_specs = (
        P("cell", "gene"),
        P(("cell", "gene"), None),
        P(("gene", "cell"), None),
        P("cell"),
        P("gene"),
    )
    out_specs = (P(("cell", "gene"), None), P(("gene", "cell"), None))
    per_device = plain_sweeps
    if (n_cell, n_gene) == (8, 4):
        per_device = functools.partial(overlapped, n_cell=n_cell, n_gene=n_gene)
    return jax.shard_map(
        per_device, mesh=mesh, in_specs=in_specs, out_specs=out_specs, check_vma=False
    )
```

```python
import functools

import jax
import jax.numpy as jnp
from jax import lax
from jax.experimental import pallas as pl
from jax.experimental.pallas import tpu as pltpu
from jax.sharding import PartitionSpec as P

ITERS = 2
LOG2E = 1.4426950408889634
BF = jnp.bfloat16
F32 = jnp.float32
NT = (((1,), (1,)), ((), ()))

epsilon = 1e-06
step_cap = 0.25


def bounded(ratio):
    return step_cap * jnp.tanh(ratio / step_cap)


def params(megabytes=14):
    return pltpu.CompilerParams(vmem_limit_bytes=megabytes * 2**20)


def pack(rows):
    half = rows.shape[0] // 2
    return jnp.concatenate([rows[:half], rows[half:]], axis=1)


def left_lanes(shape):
    return lax.broadcasted_iota(jnp.int32, shape, 1) < 64


def doubled(packed):
    turned = pltpu.roll(packed, 64, 1)
    left = left_lanes(packed.shape)
    return jnp.concatenate(
        [jnp.where(left, packed, turned), jnp.where(left, turned, packed)], axis=0
    )


def parts(x):
    hi = x.astype(BF).astype(F32)
    return hi, x - hi


def pick(left, a, b):
    return jnp.where(left, a, b).astype(BF)


def queries(x, offset):
    left = left_lanes(x.shape)
    hi, lo = parts(x * LOG2E)
    return jnp.concatenate([pick(left, hi, lo), pick(left, hi, offset.astype(F32))], axis=1)


def keys(x, offset):
    left = left_lanes(x.shape)
    hi, lo = parts(x)
    return jnp.concatenate([hi.astype(BF), pick(left, lo, offset.astype(F32))], axis=1)


def weights(x):
    left = left_lanes(x.shape)
    hi, lo = parts(x)
    square_hi, square_lo = parts(x * x)
    both = jnp.concatenate([pick(left, hi, square_hi), pick(left, lo, square_lo)], axis=1)
    grad = jnp.concatenate([pick(left, -hi, 0.0), pick(left, -lo, 0.0)], axis=1)
    return both, grad


def sums(query, key, weight, count, count_weight):
    linear = lax.dot_general(query, key, NT, preferred_element_type=F32)
    means = jnp.exp2(linear)
    hi = means.astype(BF)
    lo = (means - hi.astype(F32)).astype(BF)
    total = jnp.dot(
        jnp.concatenate([hi, lo, count], axis=1),
        jnp.concatenate([weight, weight, count_weight], axis=0),
        preferred_element_type=F32,
    )
    return total[:, :128] + total[:, 128:]


def columns_kernel(is_cell, offset_ref, out_ref):
    hi, rest = parts(offset_ref[...] * LOG2E)
    mid, low = parts(rest)
    shape = (128, offset_ref.shape[1])
    row = lax.broadcasted_iota(jnp.int32, shape, 0)
    first, ones = (64, 67) if is_cell else (67, 64)
    lines = jnp.where((row >= ones) & (row < ones + 3), 1.0, 0.0)
    for at, part in enumerate((hi, mid, low)):
        lines = jnp.where(row == first + at, part, lines)
    out_ref[...] = lines.T.astype(BF)


def columns_call(offset, is_cell):
    size = offset.shape[0]
    return pl.pallas_call(
        functools.partial(columns_kernel, is_cell),
        out_shape=jax.ShapeDtypeStruct((size, 128), BF),
        compiler_params=params(),
        cost_estimate=work(0, 0),
    )(offset.reshape(1, size))


def count_kernel(tile, where, count_ref, plain_ref, turned_ref):
    at = pl.ds(pl.multiple_of(pl.program_id(0) * tile, tile), tile)
    x = count_ref[...].astype(F32).astype(BF)
    plain_ref[:, at] = x
    turned_ref[at, :] = x.T


def count_call(where, counts, blocks=2, tile=512):
    cells, genes = counts.shape
    genes = genes // blocks
    steps = genes // tile
    return pl.pallas_call(
        functools.partial(count_kernel, tile),
        grid_spec=pltpu.PrefetchScalarGridSpec(
            num_scalar_prefetch=1,
            grid=(steps,),
            in_specs=[pl.BlockSpec((cells, tile), lambda j, w: (0, w[0] * steps + j))],
            out_specs=[pl.BlockSpec(memory_space=pltpu.VMEM)] * 2,
        ),
        out_shape=[
            jax.ShapeDtypeStruct((cells, genes), BF),
            jax.ShapeDtypeStruct((genes, cells), BF),
        ],
        compiler_params=params(42),
        cost_estimate=pl.CostEstimate(flops=0, bytes_accessed=cells * genes * 6, transcendentals=0),
    )(where, counts)


def work(cells, genes):
    return pl.CostEstimate(
        flops=2 * cells * genes * 256 * 4,
        bytes_accessed=2 * cells * genes,
        transcendentals=cells * genes,
    )


def factor_rows(core, mine_ref, other_ref):
    mine, other = mine_ref[...], other_ref[...]
    first = jnp.where(core == 0, mine, other)
    second = jnp.where(core == 0, other, mine)
    return doubled(jnp.concatenate([first, second], axis=0))


def chunk_base(where, slot, place, size):
    at = (jnp.bitwise_xor(where[1], slot) * 2 + place) * size
    return pl.multiple_of(at, size)


def factor_kernel(last, where, mine_u, other_u, cell_ref, v0, w0, v1, w1, gene_ref, count_ref, turned_ref, *rest):
    y, core = where[2], where[3]
    if last:
        sum_ref, keep_ref, send_ref, query_ref = rest
    else:
        out_ref, query_ref = rest
    query_ref[...] = queries(factor_rows(core, mine_u, other_u), cell_ref[...])
    size = v0.shape[0] * 2
    chunks = []
    for slot, refs in enumerate(((v0, w0), (v1, w1))):
        for place, ref in zip((y, 1 - y), refs):
            base = chunk_base(where, slot, place, size)
            v = doubled(ref[...])
            at = pl.ds(base, size)
            chunks.append((at, keys(v, gene_ref[at, :]), *weights(v)))
    rows = mine_u.shape[0]

    def partial_sums(row):
        span = pl.ds(row, rows)
        query = query_ref[span, :]
        total = sum_ref[span, :] if last else None
        for at, key, weight, count_weight in chunks:
            part = sums(query, key, weight, count_ref[span, at], count_weight)
            total = part if total is None else total + part
        return total

    for side in range(2):
        if last:
            for target, place in ((send_ref, 1 - core), (keep_ref, core)):
                row = pl.multiple_of(side * 2 * rows + place * rows, rows)
                target[side * rows : (side + 1) * rows, :] = partial_sums(row)
        else:
            for row in (side * 2 * rows, side * 2 * rows + rows):
                out_ref[row : row + rows, :] = partial_sums(row)


def block_specs(arrays):
    return [pl.BlockSpec(a.shape, lambda j, w: (0, 0)) for a in arrays]


def factor_call(where, u, cell_columns, v, gene_columns, counts, total=None):
    cells = counts[0].shape[0]
    tile = 8 * v[0].shape[0]
    last = total is not None
    whole = [*u, cell_columns, *v]
    extra = [total] if last else []
    shapes = [(cells // 2, 128)] * 2 if last else [(cells, 128)]
    return pl.pallas_call(
        functools.partial(factor_kernel, last),
        grid_spec=pltpu.PrefetchScalarGridSpec(
            num_scalar_prefetch=1,
            grid=(1,),
            in_specs=block_specs(whole)
            + [
                pl.BlockSpec((tile, 128), lambda j, w: (w[0], 0)),
                pl.BlockSpec(memory_space=pltpu.VMEM),
                pl.BlockSpec(memory_space=pl.ANY),
            ]
            + block_specs(extra),
            out_specs=[pl.BlockSpec(shape, lambda j, w: (0, 0)) for shape in shapes],
            scratch_shapes=[pltpu.VMEM((cells, 256), BF)],
        ),
        out_shape=[jax.ShapeDtypeStruct(shape, F32) for shape in shapes],
        compiler_params=params(),
        cost_estimate=work(cells, tile),
    )(where, *whole, gene_columns, *counts, *extra)


def opening_kernel(
    where, mine_u, other_u, cell_ref, v0, w0, v1, w1, gene_ref, count_ref, turned_ref, raw_ref,
    out_ref, plain_out, turned_out, query_ref, key_ref, weight_ref, grad_ref,
):
    y, core = where[2], where[3]
    step = pl.program_id(0)
    size = v0.shape[0] * 2
    rows = mine_u.shape[0]
    places = [(slot, place) for slot in range(2) for place in (y, 1 - y)]

    @pl.when(step == 0)
    def _():
        query_ref[...] = queries(factor_rows(core, mine_u, other_u), cell_ref[...])
        for i, (at, ref) in enumerate(zip(places, (v0, w0, v1, w1))):
            v = doubled(ref[...])
            key_ref[i] = keys(v, gene_ref[pl.ds(chunk_base(where, *at, size), size), :])
            weight_ref[i], grad_ref[i] = weights(v)

    span = pl.ds(pl.multiple_of(step * rows, rows), rows)
    total = None
    for i, at in enumerate(places):
        count = count_ref[span, pl.ds(chunk_base(where, *at, size), size)]
        part = sums(query_ref[span, :], key_ref[i], weight_ref[i], count, grad_ref[i])
        total = part if total is None else total + part
    out_ref[span, :] = total
    columns = pl.ds(pl.multiple_of(step * size, size), size)
    x = raw_ref[...].astype(F32).astype(BF)
    plain_out[:, columns] = x
    turned_out[columns, :] = x.T


def opening_call(where, u, cell_columns, v, gene_columns, counts, raw):
    cells = raw.shape[0]
    size = 2 * v[0].shape[0]
    tile = 4 * size
    whole = [*u, cell_columns, *v]
    out_shape = [
        jax.ShapeDtypeStruct((cells, 128), F32),
        jax.ShapeDtypeStruct((cells, tile), BF),
        jax.ShapeDtypeStruct((tile, cells), BF),
    ]
    return pl.pallas_call(
        opening_kernel,
        grid_spec=pltpu.PrefetchScalarGridSpec(
            num_scalar_prefetch=1,
            grid=(4,),
            in_specs=block_specs(whole)
            + [
                pl.BlockSpec((tile, 128), lambda j, w: (w[0], 0)),
                pl.BlockSpec(memory_space=pltpu.VMEM),
                pl.BlockSpec(memory_space=pl.ANY),
                pl.BlockSpec((cells, size), lambda j, w: (0, (1 - w[0]) * 4 + j)),
            ],
            out_specs=[pl.BlockSpec((cells, 128), lambda j, w: (0, 0))]
            + [pl.BlockSpec(memory_space=pltpu.VMEM)] * 2,
            scratch_shapes=[pltpu.VMEM((cells, 256), BF)] + [pltpu.VMEM((4, size, 256), BF)] * 3,
        ),
        out_shape=out_shape,
        compiler_params=params(34),
        cost_estimate=work(cells, tile),
    )(where, *whole, gene_columns, *counts, raw)


def loading_kernel(pieces, slots, where, mine_u, other_u, cell_ref, *rest):
    y, core = where[2], where[3]
    count = 2 * len(slots)
    v, (gene_ref, turned_ref), outs = rest[:count], rest[count:][:2], iter(rest[count + 2 :])
    u = factor_rows(core, mine_u, other_u)
    key = keys(u, cell_ref[...])
    weight, count_weight = weights(u)
    size = v[0].shape[0] * 2
    rows = size // 2
    for i, slot in enumerate(slots):
        for place, ref in ((1 - y, v[2 * i + 1]), (y, v[2 * i])):
            base = chunk_base(where, slot, place, size)
            query = queries(doubled(ref[...]), gene_ref[pl.ds(base, size), :])
            for half in range(2):
                if half == 0 or pieces == 2:
                    target = next(outs)
                row = half * rows if pieces == 1 else 0
                part = turned_ref[pl.ds(pl.multiple_of(base + half * rows, rows), rows), :]
                span = slice(half * rows, (half + 1) * rows)
                target[row : row + rows, :] = sums(query[span], key, weight, part, count_weight)


def loading_call(where, u, cell_columns, v, slots, gene_columns, turned, pieces):
    cells = turned.shape[1]
    half = v[0].shape[0]
    v = [part for slot in slots for part in v[2 * slot : 2 * slot + 2]]
    whole = [*u, cell_columns, *v]
    shapes = [(2 * half // pieces, 128)] * (2 * len(slots) * pieces)
    return pl.pallas_call(
        functools.partial(loading_kernel, pieces, slots),
        grid_spec=pltpu.PrefetchScalarGridSpec(
            num_scalar_prefetch=1,
            grid=(1,),
            in_specs=block_specs(whole)
            + [
                pl.BlockSpec((8 * half, 128), lambda j, w: (w[0], 0)),
                pl.BlockSpec(memory_space=pltpu.VMEM),
            ],
            out_specs=[pl.BlockSpec(shape, lambda j, w: (0, 0)) for shape in shapes],
        ),
        out_shape=[jax.ShapeDtypeStruct(shape, F32) for shape in shapes],
        compiler_params=params(),
        cost_estimate=work(cells, 4 * half * len(slots)),
    )(where, *whole, gene_columns, turned)


def stepped(packed, total):
    half = packed.shape[0]
    step = bounded(total[:, :64] / (total[:, 64:] + epsilon))
    return packed - jnp.concatenate([step[:half], step[half:]], axis=1)


def swap(x, axis, size, mask):
    return lax.ppermute(x, axis, [(i, i ^ mask) for i in range(size)])


def after(value, *others):
    return lax.optimization_barrier((value, *others))[0]


def overlapped(counts, factors, loadings, cell_offset, gene_offset, n_cell, n_gene):
    cell = lax.axis_index("cell")
    gene = lax.axis_index("gene")
    core, x = gene % 2, gene // 2
    y, z = cell % 2, cell // 2

    def over_cell(value, mask):
        return swap(value, "cell", n_cell, mask)

    def over_gene(value, mask):
        return swap(value, "gene", n_gene, mask)

    def gather_loadings(own):
        mine = [own] + [over_cell(own, 2 * s) for s in range(1, 4)]
        other = [over_cell(m, 1) for m in mine]
        return (mine[0], other[0], mine[1], other[1]), (mine[2], other[2], mine[3], other[3])

    own_v = pack(loadings)
    theirs = over_gene(factors, 2)
    own_u = jnp.where(
        x == 0,
        jnp.concatenate([factors, theirs], axis=1),
        jnp.concatenate([theirs, factors], axis=1),
    )
    u = (own_u, over_gene(own_u, 1))
    near, far = gather_loadings(own_v)
    cell_columns = columns_call(cell_offset, True)
    gene_columns = columns_call(gene_offset, False)
    near_at = jnp.stack([z // 2, z % 2, y, core])
    far_at = jnp.stack([(z // 2) ^ 1, z % 2, y, core])
    near_counts = far_counts = None

    for iteration in range(ITERS):
        if iteration == 0:
            near_counts = count_call(near_at, counts)
        if iteration == 0:
            total, *far_counts = opening_call(
                near_at, u, cell_columns, near, gene_columns, near_counts, counts
            )
        else:
            (total,) = factor_call(near_at, u, cell_columns, near, gene_columns, near_counts)
        keep, send = factor_call(far_at, u, cell_columns, far, gene_columns, far_counts, total)
        keep = keep + over_gene(send, 1)
        keep = keep + over_gene(keep, 2)
        own_u = stepped(own_u, keep)
        u = (own_u, over_gene(own_u, 1))

        def sums_of(at, v, slots, block, pieces):
            return loading_call(at, u, cell_columns, v, slots, gene_columns, block[1], pieces)

        o3a, o3b, m3a, m3b = sums_of(far_at, far, (1,), far_counts, 2)
        o3a, o3b = over_cell(o3a, 1), over_cell(o3b, 1)
        o2a, o2b, m2a, m2b = sums_of(after(far_at, m3a), far, (0,), far_counts, 2)
        o2a, o2b = over_cell(o2a, 1), over_cell(o2b, 1)
        m3a = m3a + o3a
        o1, m1, o0, m0 = sums_of(after(near_at, m3a, m2a), near, (1, 0), near_counts, 1)
        m3a, m3b = over_cell(m3a, 2), over_cell(m3b + o3b, 2)
        m2a, m2b = over_cell(m2a + o2a + m3a, 4), over_cell(m2b + o2b + m3b, 4)
        m1 = over_cell(m1 + over_cell(o1, 1), 2)
        m0 = m0 + over_cell(o0, 1)
        own_v = stepped(own_v, m0 + m1 + jnp.concatenate([m2a, m2b], axis=0))
        if iteration + 1 < ITERS:
            near, far = gather_loadings(own_v)

    new_u = jnp.where(x == 0, own_u[:, :64], own_u[:, 64:])
    new_v = jnp.concatenate([own_v[:, :64], own_v[:, 64:]], axis=0)
    return new_u, new_v


def predict(factor_rows, loading_rows, cell_part, gene_part, count_part):
    linear = jnp.dot(
        factor_rows,
        loading_rows.T,
        preferred_element_type=jnp.float32,
        precision=lax.Precision.HIGHEST,
    )
    linear = linear + cell_part[:, None] + gene_part[None, :]
    means = jnp.exp(linear)
    excess = means - count_part.astype(jnp.float32)
    return (means, excess)


def plain_sweeps(counts, factors, loadings, cell_offset, gene_offset):
    rank = factors.shape[1]
    precise = dict(preferred_element_type=F32, precision=lax.Precision.HIGHEST)
    contract = (((0,), (0,)), ((), ()))
    own_u, own_v = factors, loadings
    u = lax.all_gather(own_u, "gene", axis=0, tiled=True)
    v = lax.all_gather(own_v, "cell", axis=0, tiled=True)
    for iteration in range(ITERS):
        means, excess = predict(u, v, cell_offset, gene_offset, counts)
        grad = jnp.dot(excess, v, **precise)
        curv = jnp.dot(means, v * v, **precise)
        shares = lax.psum_scatter(
            jnp.concatenate([grad, curv], axis=1), "gene", scatter_dimension=0, tiled=True
        )
        own_u = own_u - bounded(shares[:, :rank] / (shares[:, rank:] + epsilon))
        u = lax.all_gather(own_u, "gene", axis=0, tiled=True)
        means, excess = predict(u, v, cell_offset, gene_offset, counts)
        grad = lax.dot_general(excess, u, contract, **precise)
        curv = lax.dot_general(means, u * u, contract, **precise)
        shares = lax.psum_scatter(
            jnp.concatenate([grad, curv], axis=1), "cell", scatter_dimension=0, tiled=True
        )
        own_v = own_v - bounded(shares[:, :rank] / (shares[:, rank:] + epsilon))
        if iteration + 1 < ITERS:
            v = lax.all_gather(own_v, "cell", axis=0, tiled=True)
    return own_u, own_v


def solution(mesh):
    n_cell, n_gene = mesh.shape["cell"], mesh.shape["gene"]
    in_specs = (
        P("cell", "gene"),
        P(("cell", "gene"), None),
        P(("gene", "cell"), None),
        P("cell"),
        P("gene"),
    )
    out_specs = (P(("cell", "gene"), None), P(("gene", "cell"), None))
    per_device = plain_sweeps
    if (n_cell, n_gene) == (8, 4):
        per_device = functools.partial(overlapped, n_cell=n_cell, n_gene=n_gene)
    return jax.shard_map(
        per_device, mesh=mesh, in_specs=in_specs, out_specs=out_specs, check_vma=False
    )
```

```python
import functools

import jax
import jax.numpy as jnp
from jax import lax
from jax.experimental import pallas as pl
from jax.experimental.pallas import tpu as pltpu
from jax.sharding import PartitionSpec as P

ITERS = 2
LOG2E = 1.4426950408889634
BF = jnp.bfloat16
F32 = jnp.float32
NT = (((1,), (1,)), ((), ()))

epsilon = 1e-06
step_cap = 0.25


def bounded(ratio):
    return step_cap * jnp.tanh(ratio / step_cap)


def params(megabytes=14):
    return pltpu.CompilerParams(vmem_limit_bytes=megabytes * 2**20)


def pack(rows):
    half = rows.shape[0] // 2
    return jnp.concatenate([rows[:half], rows[half:]], axis=1)


def left_lanes(shape):
    return lax.broadcasted_iota(jnp.int32, shape, 1) < 64


def doubled(packed):
    turned = pltpu.roll(packed, 64, 1)
    left = left_lanes(packed.shape)
    return jnp.concatenate(
        [jnp.where(left, packed, turned), jnp.where(left, turned, packed)], axis=0
    )


def parts(x):
    hi = x.astype(BF).astype(F32)
    return hi, x - hi


def pick(left, a, b):
    return jnp.where(left, a, b).astype(BF)


def queries(x, offset):
    left = left_lanes(x.shape)
    hi, lo = parts(x * LOG2E)
    return jnp.concatenate([pick(left, hi, lo), pick(left, hi, offset.astype(F32))], axis=1)


def keys(x, offset):
    left = left_lanes(x.shape)
    hi, lo = parts(x)
    return jnp.concatenate([hi.astype(BF), pick(left, lo, offset.astype(F32))], axis=1)


def weights(x):
    left = left_lanes(x.shape)
    hi, lo = parts(x)
    square_hi, square_lo = parts(x * x)
    both = jnp.concatenate([pick(left, hi, square_hi), pick(left, lo, square_lo)], axis=1)
    grad = jnp.concatenate([pick(left, -hi, 0.0), pick(left, -lo, 0.0)], axis=1)
    return both, grad


def sums(query, key, weight, count, count_weight):
    linear = lax.dot_general(query, key, NT, preferred_element_type=F32)
    means = jnp.exp2(linear)
    hi = means.astype(BF)
    lo = (means - hi.astype(F32)).astype(BF)
    total = jnp.dot(
        jnp.concatenate([hi, lo, count], axis=1),
        jnp.concatenate([weight, weight, count_weight], axis=0),
        preferred_element_type=F32,
    )
    return total[:, :128] + total[:, 128:]


def columns_kernel(is_cell, offset_ref, out_ref):
    hi, rest = parts(offset_ref[...] * LOG2E)
    mid, low = parts(rest)
    shape = (128, offset_ref.shape[1])
    row = lax.broadcasted_iota(jnp.int32, shape, 0)
    first, ones = (64, 67) if is_cell else (67, 64)
    lines = jnp.where((row >= ones) & (row < ones + 3), 1.0, 0.0)
    for at, part in enumerate((hi, mid, low)):
        lines = jnp.where(row == first + at, part, lines)
    out_ref[...] = lines.T.astype(BF)


def columns_call(offset, is_cell):
    size = offset.shape[0]
    return pl.pallas_call(
        functools.partial(columns_kernel, is_cell),
        out_shape=jax.ShapeDtypeStruct((size, 128), BF),
        compiler_params=params(),
        cost_estimate=work(0, 0),
    )(offset.reshape(1, size))


def count_kernel(tile, where, count_ref, plain_ref, turned_ref):
    at = pl.ds(pl.multiple_of(pl.program_id(0) * tile, tile), tile)
    x = count_ref[...].astype(F32).astype(BF)
    plain_ref[:, at] = x
    turned_ref[at, :] = x.T


def count_call(where, counts, blocks=2, tile=512):
    cells, genes = counts.shape
    genes = genes // blocks
    steps = genes // tile
    return pl.pallas_call(
        functools.partial(count_kernel, tile),
        grid_spec=pltpu.PrefetchScalarGridSpec(
            num_scalar_prefetch=1,
            grid=(steps,),
            in_specs=[pl.BlockSpec((cells, tile), lambda j, w: (0, w[0] * steps + j))],
            out_specs=[pl.BlockSpec(memory_space=pltpu.VMEM)] * 2,
        ),
        out_shape=[
            jax.ShapeDtypeStruct((cells, genes), BF),
            jax.ShapeDtypeStruct((genes, cells), BF),
        ],
        compiler_params=params(42),
        cost_estimate=pl.CostEstimate(flops=0, bytes_accessed=cells * genes * 6, transcendentals=0),
    )(where, counts)


def work(cells, genes):
    return pl.CostEstimate(
        flops=2 * cells * genes * 256 * 4,
        bytes_accessed=2 * cells * genes,
        transcendentals=cells * genes,
    )


def factor_rows(core, mine_ref, other_ref):
    mine, other = mine_ref[...], other_ref[...]
    first = jnp.where(core == 0, mine, other)
    second = jnp.where(core == 0, other, mine)
    return doubled(jnp.concatenate([first, second], axis=0))


def chunk_base(where, slot, place, size):
    at = (jnp.bitwise_xor(where[1], slot) * 2 + place) * size
    return pl.multiple_of(at, size)


def factor_kernel(last, where, mine_u, other_u, cell_ref, v0, w0, v1, w1, gene_ref, count_ref, turned_ref, *rest):
    y, core = where[2], where[3]
    if last:
        sum_ref, keep_ref, send_ref, query_ref = rest
    else:
        out_ref, query_ref = rest
    query_ref[...] = queries(factor_rows(core, mine_u, other_u), cell_ref[...])
    size = v0.shape[0] * 2
    chunks = []
    for slot, refs in enumerate(((v0, w0), (v1, w1))):
        for place, ref in zip((y, 1 - y), refs):
            base = chunk_base(where, slot, place, size)
            v = doubled(ref[...])
            at = pl.ds(base, size)
            chunks.append((at, keys(v, gene_ref[at, :]), *weights(v)))
    rows = mine_u.shape[0]

    def partial_sums(row):
        span = pl.ds(row, rows)
        query = query_ref[span, :]
        total = sum_ref[span, :] if last else None
        for at, key, weight, count_weight in chunks:
            part = sums(query, key, weight, count_ref[span, at], count_weight)
            total = part if total is None else total + part
        return total

    for side in range(2):
        if last:
            for target, place in ((send_ref, 1 - core), (keep_ref, core)):
                row = pl.multiple_of(side * 2 * rows + place * rows, rows)
                target[side * rows : (side + 1) * rows, :] = partial_sums(row)
        else:
            for row in (side * 2 * rows, side * 2 * rows + rows):
                out_ref[row : row + rows, :] = partial_sums(row)


def block_specs(arrays):
    return [pl.BlockSpec(a.shape, lambda j, w: (0, 0)) for a in arrays]


def factor_call(where, u, cell_columns, v, gene_columns, counts, total=None):
    cells = counts[0].shape[0]
    tile = 8 * v[0].shape[0]
    last = total is not None
    whole = [*u, cell_columns, *v]
    extra = [total] if last else []
    shapes = [(cells // 2, 128)] * 2 if last else [(cells, 128)]
    return pl.pallas_call(
        functools.partial(factor_kernel, last),
        grid_spec=pltpu.PrefetchScalarGridSpec(
            num_scalar_prefetch=1,
            grid=(1,),
            in_specs=block_specs(whole)
            + [
                pl.BlockSpec((tile, 128), lambda j, w: (w[0], 0)),
                pl.BlockSpec(memory_space=pltpu.VMEM),
                pl.BlockSpec(memory_space=pl.ANY),
            ]
            + block_specs(extra),
            out_specs=[pl.BlockSpec(shape, lambda j, w: (0, 0)) for shape in shapes],
            scratch_shapes=[pltpu.VMEM((cells, 256), BF)],
        ),
        out_shape=[jax.ShapeDtypeStruct(shape, F32) for shape in shapes],
        compiler_params=params(),
        cost_estimate=work(cells, tile),
    )(where, *whole, gene_columns, *counts, *extra)


def opening_kernel(
    where, mine_u, other_u, cell_ref, v0, w0, v1, w1, gene_ref, count_ref, turned_ref, raw_ref,
    out_ref, plain_out, turned_out, query_ref, key_ref, weight_ref, grad_ref,
):
    y, core = where[2], where[3]
    step = pl.program_id(0)
    size = v0.shape[0] * 2
    rows = mine_u.shape[0]
    places = [(slot, place) for slot in range(2) for place in (y, 1 - y)]

    @pl.when(step == 0)
    def _():
        query_ref[...] = queries(factor_rows(core, mine_u, other_u), cell_ref[...])
        for i, (at, ref) in enumerate(zip(places, (v0, w0, v1, w1))):
            v = doubled(ref[...])
            key_ref[i] = keys(v, gene_ref[pl.ds(chunk_base(where, *at, size), size), :])
            weight_ref[i], grad_ref[i] = weights(v)

    span = pl.ds(pl.multiple_of(step * rows, rows), rows)
    total = None
    for i, at in enumerate(places):
        count = count_ref[span, pl.ds(chunk_base(where, *at, size), size)]
        part = sums(query_ref[span, :], key_ref[i], weight_ref[i], count, grad_ref[i])
        total = part if total is None else total + part
    out_ref[span, :] = total
    columns = pl.ds(pl.multiple_of(step * size, size), size)
    x = raw_ref[...].astype(F32).astype(BF)
    plain_out[:, columns] = x
    turned_out[columns, :] = x.T


def opening_call(where, u, cell_columns, v, gene_columns, counts, raw):
    cells = raw.shape[0]
    size = 2 * v[0].shape[0]
    tile = 4 * size
    whole = [*u, cell_columns, *v]
    out_shape = [
        jax.ShapeDtypeStruct((cells, 128), F32),
        jax.ShapeDtypeStruct((cells, tile), BF),
        jax.ShapeDtypeStruct((tile, cells), BF),
    ]
    return pl.pallas_call(
        opening_kernel,
        grid_spec=pltpu.PrefetchScalarGridSpec(
            num_scalar_prefetch=1,
            grid=(4,),
            in_specs=block_specs(whole)
            + [
                pl.BlockSpec((tile, 128), lambda j, w: (w[0], 0)),
                pl.BlockSpec(memory_space=pltpu.VMEM),
                pl.BlockSpec(memory_space=pl.ANY),
                pl.BlockSpec((cells, size), lambda j, w: (0, (1 - w[0]) * 4 + j)),
            ],
            out_specs=[pl.BlockSpec((cells, 128), lambda j, w: (0, 0))]
            + [pl.BlockSpec(memory_space=pltpu.VMEM)] * 2,
            scratch_shapes=[pltpu.VMEM((cells, 256), BF)] + [pltpu.VMEM((4, size, 256), BF)] * 3,
        ),
        out_shape=out_shape,
        compiler_params=params(34),
        cost_estimate=work(cells, tile),
    )(where, *whole, gene_columns, *counts, raw)


def loading_kernel(pieces, slots, where, mine_u, other_u, cell_ref, *rest):
    y, core = where[2], where[3]
    count = 2 * len(slots)
    v, (gene_ref, turned_ref), outs = rest[:count], rest[count:][:2], iter(rest[count + 2 :])
    u = factor_rows(core, mine_u, other_u)
    key = keys(u, cell_ref[...])
    weight, count_weight = weights(u)
    size = v[0].shape[0] * 2
    rows = size // 2
    for i, slot in enumerate(slots):
        for place, ref in ((1 - y, v[2 * i + 1]), (y, v[2 * i])):
            base = chunk_base(where, slot, place, size)
            query = queries(doubled(ref[...]), gene_ref[pl.ds(base, size), :])
            for half in range(2):
                if half == 0 or pieces == 2:
                    target = next(outs)
                row = half * rows if pieces == 1 else 0
                part = turned_ref[pl.ds(pl.multiple_of(base + half * rows, rows), rows), :]
                span = slice(half * rows, (half + 1) * rows)
                target[row : row + rows, :] = sums(query[span], key, weight, part, count_weight)


def loading_call(where, u, cell_columns, v, slots, gene_columns, turned, pieces):
    cells = turned.shape[1]
    half = v[0].shape[0]
    v = [part for slot in slots for part in v[2 * slot : 2 * slot + 2]]
    whole = [*u, cell_columns, *v]
    shapes = [(2 * half // pieces, 128)] * (2 * len(slots) * pieces)
    return pl.pallas_call(
        functools.partial(loading_kernel, pieces, slots),
        grid_spec=pltpu.PrefetchScalarGridSpec(
            num_scalar_prefetch=1,
            grid=(1,),
            in_specs=block_specs(whole)
            + [
                pl.BlockSpec((8 * half, 128), lambda j, w: (w[0], 0)),
                pl.BlockSpec(memory_space=pltpu.VMEM),
            ],
            out_specs=[pl.BlockSpec(shape, lambda j, w: (0, 0)) for shape in shapes],
        ),
        out_shape=[jax.ShapeDtypeStruct(shape, F32) for shape in shapes],
        compiler_params=params(),
        cost_estimate=work(cells, 4 * half * len(slots)),
    )(where, *whole, gene_columns, turned)


def stepped(packed, total):
    half = packed.shape[0]
    step = bounded(total[:, :64] / (total[:, 64:] + epsilon))
    return packed - jnp.concatenate([step[:half], step[half:]], axis=1)


def swap(x, axis, size, mask):
    return lax.ppermute(x, axis, [(i, i ^ mask) for i in range(size)])


def after(value, *others):
    return lax.optimization_barrier((value, *others))[0]


def overlapped(counts, factors, loadings, cell_offset, gene_offset, n_cell, n_gene):
    cell = lax.axis_index("cell")
    gene = lax.axis_index("gene")
    core, x = gene % 2, gene // 2
    y, z = cell % 2, cell // 2

    def over_cell(value, mask):
        return swap(value, "cell", n_cell, mask)

    def over_gene(value, mask):
        return swap(value, "gene", n_gene, mask)

    def gather_loadings(own):
        mine = [own] + [over_cell(own, 2 * s) for s in range(1, 4)]
        other = [over_cell(m, 1) for m in mine]
        return (mine[0], other[0], mine[1], other[1]), (mine[2], other[2], mine[3], other[3])

    own_v = pack(loadings)
    theirs = over_gene(factors, 2)
    own_u = jnp.where(
        x == 0,
        jnp.concatenate([factors, theirs], axis=1),
        jnp.concatenate([theirs, factors], axis=1),
    )
    u = (own_u, over_gene(own_u, 1))
    near, far = gather_loadings(own_v)
    cell_columns = columns_call(cell_offset, True)
    gene_columns = columns_call(gene_offset, False)
    near_at = jnp.stack([z // 2, z % 2, y, core])
    far_at = jnp.stack([(z // 2) ^ 1, z % 2, y, core])
    near_counts = far_counts = None

    for iteration in range(ITERS):
        if iteration == 0:
            near_counts = count_call(near_at, counts)
        if iteration == 0:
            total, *far_counts = opening_call(
                near_at, u, cell_columns, near, gene_columns, near_counts, counts
            )
        else:
            (total,) = factor_call(near_at, u, cell_columns, near, gene_columns, near_counts)
        keep, send = factor_call(far_at, u, cell_columns, far, gene_columns, far_counts, total)
        keep = keep + over_gene(send, 1)
        keep = keep + over_gene(keep, 2)
        own_u = stepped(own_u, keep)
        u = (own_u, over_gene(own_u, 1))

        def sums_of(at, v, slots, block, pieces):
            return loading_call(at, u, cell_columns, v, slots, gene_columns, block[1], pieces)

        o3a, o3b, m3a, m3b = sums_of(far_at, far, (1,), far_counts, 2)
        o3a, o3b = over_cell(o3a, 1), over_cell(o3b, 1)
        o2a, o2b, m2a, m2b = sums_of(after(far_at, m3a), far, (0,), far_counts, 2)
        o2a, o2b = over_cell(o2a, 1), over_cell(o2b, 1)
        m3a = m3a + o3a
        o1, m1 = sums_of(after(near_at, m3a, m2a), near, (1,), near_counts, 1)
        o1 = over_cell(o1, 1)
        m3a, m3b = over_cell(m3a, 2), over_cell(m3b + o3b, 2)
        m2a, m2b = m2a + o2a + m3a, m2b + o2b + m3b
        o0, m0 = sums_of(after(near_at, m2b, m1), near, (0,), near_counts, 1)
        m2a, m2b = over_cell(m2a, 4), over_cell(m2b, 4)
        m1 = over_cell(m1 + o1, 2)
        m0 = m0 + over_cell(o0, 1)
        own_v = stepped(own_v, m0 + m1 + jnp.concatenate([m2a, m2b], axis=0))
        if iteration + 1 < ITERS:
            near, far = gather_loadings(own_v)

    new_u = jnp.where(x == 0, own_u[:, :64], own_u[:, 64:])
    new_v = jnp.concatenate([own_v[:, :64], own_v[:, 64:]], axis=0)
    return new_u, new_v


def predict(factor_rows, loading_rows, cell_part, gene_part, count_part):
    linear = jnp.dot(
        factor_rows,
        loading_rows.T,
        preferred_element_type=jnp.float32,
        precision=lax.Precision.HIGHEST,
    )
    linear = linear + cell_part[:, None] + gene_part[None, :]
    means = jnp.exp(linear)
    excess = means - count_part.astype(jnp.float32)
    return (means, excess)


def plain_sweeps(counts, factors, loadings, cell_offset, gene_offset):
    rank = factors.shape[1]
    precise = dict(preferred_element_type=F32, precision=lax.Precision.HIGHEST)
    contract = (((0,), (0,)), ((), ()))
    own_u, own_v = factors, loadings
    u = lax.all_gather(own_u, "gene", axis=0, tiled=True)
    v = lax.all_gather(own_v, "cell", axis=0, tiled=True)
    for iteration in range(ITERS):
        means, excess = predict(u, v, cell_offset, gene_offset, counts)
        grad = jnp.dot(excess, v, **precise)
        curv = jnp.dot(means, v * v, **precise)
        shares = lax.psum_scatter(
            jnp.concatenate([grad, curv], axis=1), "gene", scatter_dimension=0, tiled=True
        )
        own_u = own_u - bounded(shares[:, :rank] / (shares[:, rank:] + epsilon))
        u = lax.all_gather(own_u, "gene", axis=0, tiled=True)
        means, excess = predict(u, v, cell_offset, gene_offset, counts)
        grad = lax.dot_general(excess, u, contract, **precise)
        curv = lax.dot_general(means, u * u, contract, **precise)
        shares = lax.psum_scatter(
            jnp.concatenate([grad, curv], axis=1), "cell", scatter_dimension=0, tiled=True
        )
        own_v = own_v - bounded(shares[:, :rank] / (shares[:, rank:] + epsilon))
        if iteration + 1 < ITERS:
            v = lax.all_gather(own_v, "cell", axis=0, tiled=True)
    return own_u, own_v


def solution(mesh):
    n_cell, n_gene = mesh.shape["cell"], mesh.shape["gene"]
    in_specs = (
        P("cell", "gene"),
        P(("cell", "gene"), None),
        P(("gene", "cell"), None),
        P("cell"),
        P("gene"),
    )
    out_specs = (P(("cell", "gene"), None), P(("gene", "cell"), None))
    per_device = plain_sweeps
    if (n_cell, n_gene) == (8, 4):
        per_device = functools.partial(overlapped, n_cell=n_cell, n_gene=n_gene)
    return jax.shard_map(
        per_device, mesh=mesh, in_specs=in_specs, out_specs=out_specs, check_vma=False
    )
```

```python
import functools

import jax
import jax.numpy as jnp
from jax import lax
from jax.experimental import pallas as pl
from jax.experimental.pallas import tpu as pltpu
from jax.sharding import PartitionSpec as P

ITERS = 2
LOG2E = 1.4426950408889634
BF = jnp.bfloat16
F32 = jnp.float32
NT = (((1,), (1,)), ((), ()))

epsilon = 1e-06
step_cap = 0.25


def bounded(ratio):
    return step_cap * jnp.tanh(ratio / step_cap)


def params(megabytes=14):
    return pltpu.CompilerParams(vmem_limit_bytes=megabytes * 2**20)


def pack(rows):
    half = rows.shape[0] // 2
    return jnp.concatenate([rows[:half], rows[half:]], axis=1)


def left_lanes(shape):
    return lax.broadcasted_iota(jnp.int32, shape, 1) < 64


def doubled(packed):
    turned = pltpu.roll(packed, 64, 1)
    left = left_lanes(packed.shape)
    return jnp.concatenate(
        [jnp.where(left, packed, turned), jnp.where(left, turned, packed)], axis=0
    )


def parts(x):
    hi = x.astype(BF).astype(F32)
    return hi, x - hi


def pick(left, a, b):
    return jnp.where(left, a, b).astype(BF)


def queries(x, offset):
    left = left_lanes(x.shape)
    hi, lo = parts(x * LOG2E)
    return jnp.concatenate([pick(left, hi, lo), pick(left, hi, offset.astype(F32))], axis=1)


def keys(x, offset):
    left = left_lanes(x.shape)
    hi, lo = parts(x)
    return jnp.concatenate([hi.astype(BF), pick(left, lo, offset.astype(F32))], axis=1)


def weights(x):
    left = left_lanes(x.shape)
    hi, lo = parts(x)
    square_hi, square_lo = parts(x * x)
    both = jnp.concatenate([pick(left, hi, square_hi), pick(left, lo, square_lo)], axis=1)
    grad = jnp.concatenate([pick(left, -hi, 0.0), pick(left, -lo, 0.0)], axis=1)
    return both, grad


def sums(query, key, weight, count, count_weight):
    linear = lax.dot_general(query, key, NT, preferred_element_type=F32)
    means = jnp.exp2(linear)
    hi = means.astype(BF)
    lo = (means - hi.astype(F32)).astype(BF)
    total = jnp.dot(
        jnp.concatenate([hi, lo, count], axis=1),
        jnp.concatenate([weight, weight, count_weight], axis=0),
        preferred_element_type=F32,
    )
    return total[:, :128] + total[:, 128:]


def columns_kernel(is_cell, offset_ref, out_ref):
    hi, rest = parts(offset_ref[...] * LOG2E)
    mid, low = parts(rest)
    shape = (128, offset_ref.shape[1])
    row = lax.broadcasted_iota(jnp.int32, shape, 0)
    first, ones = (64, 67) if is_cell else (67, 64)
    lines = jnp.where((row >= ones) & (row < ones + 3), 1.0, 0.0)
    for at, part in enumerate((hi, mid, low)):
        lines = jnp.where(row == first + at, part, lines)
    out_ref[...] = lines.T.astype(BF)


def columns_call(offset, is_cell):
    size = offset.shape[0]
    return pl.pallas_call(
        functools.partial(columns_kernel, is_cell),
        out_shape=jax.ShapeDtypeStruct((size, 128), BF),
        compiler_params=params(),
        cost_estimate=work(0, 0),
    )(offset.reshape(1, size))


def count_kernel(tile, where, count_ref, plain_ref, turned_ref):
    at = pl.ds(pl.multiple_of(pl.program_id(0) * tile, tile), tile)
    x = count_ref[...].astype(F32).astype(BF)
    plain_ref[:, at] = x
    turned_ref[at, :] = x.T


def count_call(where, counts, blocks=2, tile=512):
    cells, genes = counts.shape
    genes = genes // blocks
    steps = genes // tile
    return pl.pallas_call(
        functools.partial(count_kernel, tile),
        grid_spec=pltpu.PrefetchScalarGridSpec(
            num_scalar_prefetch=1,
            grid=(steps,),
            in_specs=[pl.BlockSpec((cells, tile), lambda j, w: (0, w[0] * steps + j))],
            out_specs=[pl.BlockSpec(memory_space=pltpu.VMEM)] * 2,
        ),
        out_shape=[
            jax.ShapeDtypeStruct((cells, genes), BF),
            jax.ShapeDtypeStruct((genes, cells), BF),
        ],
        compiler_params=params(42),
        cost_estimate=pl.CostEstimate(flops=0, bytes_accessed=cells * genes * 6, transcendentals=0),
    )(where, counts)


def work(cells, genes):
    return pl.CostEstimate(
        flops=2 * cells * genes * 256 * 4,
        bytes_accessed=2 * cells * genes,
        transcendentals=cells * genes,
    )


def factor_rows(core, mine_ref, other_ref):
    mine, other = mine_ref[...], other_ref[...]
    first = jnp.where(core == 0, mine, other)
    second = jnp.where(core == 0, other, mine)
    return doubled(jnp.concatenate([first, second], axis=0))


def chunk_base(where, slot, place, size):
    at = (jnp.bitwise_xor(where[1], slot) * 2 + place) * size
    return pl.multiple_of(at, size)


def factor_kernel(last, where, mine_u, other_u, cell_ref, v0, w0, v1, w1, gene_ref, count_ref, turned_ref, *rest):
    y, core = where[2], where[3]
    if last:
        sum_ref, keep_ref, send_ref, query_ref = rest
    else:
        out_ref, query_ref = rest
    query_ref[...] = queries(factor_rows(core, mine_u, other_u), cell_ref[...])
    size = v0.shape[0] * 2
    chunks = []
    for slot, refs in enumerate(((v0, w0), (v1, w1))):
        for place, ref in zip((y, 1 - y), refs):
            base = chunk_base(where, slot, place, size)
            v = doubled(ref[...])
            at = pl.ds(base, size)
            chunks.append((at, keys(v, gene_ref[at, :]), *weights(v)))
    rows = mine_u.shape[0]

    def partial_sums(row):
        span = pl.ds(row, rows)
        query = query_ref[span, :]
        total = sum_ref[span, :] if last else None
        for at, key, weight, count_weight in chunks:
            part = sums(query, key, weight, count_ref[span, at], count_weight)
            total = part if total is None else total + part
        return total

    for side in range(2):
        if last:
            for target, place in ((send_ref, 1 - core), (keep_ref, core)):
                row = pl.multiple_of(side * 2 * rows + place * rows, rows)
                target[side * rows : (side + 1) * rows, :] = partial_sums(row)
        else:
            for row in (side * 2 * rows, side * 2 * rows + rows):
                out_ref[row : row + rows, :] = partial_sums(row)


def block_specs(arrays):
    return [pl.BlockSpec(a.shape, lambda j, w: (0, 0)) for a in arrays]


def factor_call(where, u, cell_columns, v, gene_columns, counts, total=None):
    cells = counts[0].shape[0]
    tile = 8 * v[0].shape[0]
    last = total is not None
    whole = [*u, cell_columns, *v]
    extra = [total] if last else []
    shapes = [(cells // 2, 128)] * 2 if last else [(cells, 128)]
    return pl.pallas_call(
        functools.partial(factor_kernel, last),
        grid_spec=pltpu.PrefetchScalarGridSpec(
            num_scalar_prefetch=1,
            grid=(1,),
            in_specs=block_specs(whole)
            + [
                pl.BlockSpec((tile, 128), lambda j, w: (w[0], 0)),
                pl.BlockSpec(memory_space=pltpu.VMEM),
                pl.BlockSpec(memory_space=pl.ANY),
            ]
            + block_specs(extra),
            out_specs=[pl.BlockSpec(shape, lambda j, w: (0, 0)) for shape in shapes],
            scratch_shapes=[pltpu.VMEM((cells, 256), BF)],
        ),
        out_shape=[jax.ShapeDtypeStruct(shape, F32) for shape in shapes],
        compiler_params=params(),
        cost_estimate=work(cells, tile),
    )(where, *whole, gene_columns, *counts, *extra)


def opening_kernel(
    where, mine_u, other_u, cell_ref, v0, w0, v1, w1, gene_ref, count_ref, turned_ref, raw_ref,
    out_ref, plain_out, turned_out, query_ref, key_ref, weight_ref, grad_ref,
):
    y, core = where[2], where[3]
    step = pl.program_id(0)
    size = v0.shape[0] * 2
    rows = mine_u.shape[0]
    places = [(slot, place) for slot in range(2) for place in (y, 1 - y)]

    @pl.when(step == 0)
    def _():
        query_ref[...] = queries(factor_rows(core, mine_u, other_u), cell_ref[...])
        for i, (at, ref) in enumerate(zip(places, (v0, w0, v1, w1))):
            v = doubled(ref[...])
            key_ref[i] = keys(v, gene_ref[pl.ds(chunk_base(where, *at, size), size), :])
            weight_ref[i], grad_ref[i] = weights(v)

    span = pl.ds(pl.multiple_of(step * rows, rows), rows)
    total = None
    for i, at in enumerate(places):
        count = count_ref[span, pl.ds(chunk_base(where, *at, size), size)]
        part = sums(query_ref[span, :], key_ref[i], weight_ref[i], count, grad_ref[i])
        total = part if total is None else total + part
    out_ref[span, :] = total
    columns = pl.ds(pl.multiple_of(step * size, size), size)
    x = raw_ref[...].astype(F32).astype(BF)
    plain_out[:, columns] = x
    turned_out[columns, :] = x.T


def opening_call(where, u, cell_columns, v, gene_columns, counts, raw):
    cells = raw.shape[0]
    size = 2 * v[0].shape[0]
    tile = 4 * size
    whole = [*u, cell_columns, *v]
    out_shape = [
        jax.ShapeDtypeStruct((cells, 128), F32),
        jax.ShapeDtypeStruct((cells, tile), BF),
        jax.ShapeDtypeStruct((tile, cells), BF),
    ]
    return pl.pallas_call(
        opening_kernel,
        grid_spec=pltpu.PrefetchScalarGridSpec(
            num_scalar_prefetch=1,
            grid=(4,),
            in_specs=block_specs(whole)
            + [
                pl.BlockSpec((tile, 128), lambda j, w: (w[0], 0)),
                pl.BlockSpec(memory_space=pltpu.VMEM),
                pl.BlockSpec(memory_space=pl.ANY),
                pl.BlockSpec((cells, size), lambda j, w: (0, (1 - w[0]) * 4 + j)),
            ],
            out_specs=[pl.BlockSpec((cells, 128), lambda j, w: (0, 0))]
            + [pl.BlockSpec(memory_space=pltpu.VMEM)] * 2,
            scratch_shapes=[pltpu.VMEM((cells, 256), BF)] + [pltpu.VMEM((4, size, 256), BF)] * 3,
        ),
        out_shape=out_shape,
        compiler_params=params(34),
        cost_estimate=work(cells, tile),
    )(where, *whole, gene_columns, *counts, raw)


def loading_kernel(pieces, slots, where, mine_u, other_u, cell_ref, *rest):
    y, core = where[2], where[3]
    count = 2 * len(slots)
    v, (gene_ref, turned_ref), outs = rest[:count], rest[count:][:2], iter(rest[count + 2 :])
    u = factor_rows(core, mine_u, other_u)
    key = keys(u, cell_ref[...])
    weight, count_weight = weights(u)
    size = v[0].shape[0] * 2
    rows = size // 2
    for i, slot in enumerate(slots):
        for place, ref in ((1 - y, v[2 * i + 1]), (y, v[2 * i])):
            base = chunk_base(where, slot, place, size)
            query = queries(doubled(ref[...]), gene_ref[pl.ds(base, size), :])
            for half in range(2):
                if half == 0 or pieces == 2:
                    target = next(outs)
                row = half * rows if pieces == 1 else 0
                part = turned_ref[pl.ds(pl.multiple_of(base + half * rows, rows), rows), :]
                span = slice(half * rows, (half + 1) * rows)
                target[row : row + rows, :] = sums(query[span], key, weight, part, count_weight)


def loading_call(where, u, cell_columns, v, slots, gene_columns, turned, pieces):
    cells = turned.shape[1]
    half = v[0].shape[0]
    v = [part for slot in slots for part in v[2 * slot : 2 * slot + 2]]
    whole = [*u, cell_columns, *v]
    shapes = [(2 * half // pieces, 128)] * (2 * len(slots) * pieces)
    return pl.pallas_call(
        functools.partial(loading_kernel, pieces, slots),
        grid_spec=pltpu.PrefetchScalarGridSpec(
            num_scalar_prefetch=1,
            grid=(1,),
            in_specs=block_specs(whole)
            + [
                pl.BlockSpec((8 * half, 128), lambda j, w: (w[0], 0)),
                pl.BlockSpec(memory_space=pltpu.VMEM),
            ],
            out_specs=[pl.BlockSpec(shape, lambda j, w: (0, 0)) for shape in shapes],
        ),
        out_shape=[jax.ShapeDtypeStruct(shape, F32) for shape in shapes],
        compiler_params=params(),
        cost_estimate=work(cells, 4 * half * len(slots)),
    )(where, *whole, gene_columns, turned)


def stepped(packed, total):
    half = packed.shape[0]
    step = bounded(total[:, :64] / (total[:, 64:] + epsilon))
    return packed - jnp.concatenate([step[:half], step[half:]], axis=1)


def swap(x, axis, size, mask):
    return lax.ppermute(x, axis, [(i, i ^ mask) for i in range(size)])


def after(value, *others):
    return lax.optimization_barrier((value, *others))[0]


def overlapped(counts, factors, loadings, cell_offset, gene_offset, n_cell, n_gene):
    cell = lax.axis_index("cell")
    gene = lax.axis_index("gene")
    core, x = gene % 2, gene // 2
    y, z = cell % 2, cell // 2

    def over_cell(value, mask):
        return swap(value, "cell", n_cell, mask)

    def over_gene(value, mask):
        return swap(value, "gene", n_gene, mask)

    def gather_loadings(own):
        mine = [own] + [over_cell(own, 2 * s) for s in range(1, 4)]
        other = [over_cell(m, 1) for m in mine]
        return (mine[0], other[0], mine[1], other[1]), (mine[2], other[2], mine[3], other[3])

    own_v = pack(loadings)
    theirs = over_gene(factors, 2)
    own_u = jnp.where(
        x == 0,
        jnp.concatenate([factors, theirs], axis=1),
        jnp.concatenate([theirs, factors], axis=1),
    )
    u = (own_u, over_gene(own_u, 1))
    near, far = gather_loadings(own_v)
    cell_columns = columns_call(cell_offset, True)
    gene_columns = columns_call(gene_offset, False)
    near_at = jnp.stack([z // 2, z % 2, y, core])
    far_at = jnp.stack([(z // 2) ^ 1, z % 2, y, core])
    near_counts = far_counts = None

    for iteration in range(ITERS):
        if iteration == 0:
            near_counts = count_call(near_at, counts)
        if iteration == 0:
            total, *far_counts = opening_call(
                near_at, u, cell_columns, near, gene_columns, near_counts, counts
            )
        else:
            (total,) = factor_call(near_at, u, cell_columns, near, gene_columns, near_counts)
        keep, send = factor_call(far_at, u, cell_columns, far, gene_columns, far_counts, total)
        keep = keep + over_gene(send, 1)
        keep = keep + over_gene(keep, 2)
        own_u = stepped(own_u, keep)
        u = (own_u, over_gene(own_u, 1))

        def sums_of(at, v, slots, block, pieces):
            return loading_call(at, u, cell_columns, v, slots, gene_columns, block[1], pieces)

        o3a, o3b, m3a, m3b = sums_of(far_at, far, (1,), far_counts, 2)
        o3a, o3b = over_cell(o3a, 1), over_cell(o3b, 1)
        o2a, o2b, m2a, m2b = sums_of(after(far_at, m3a), far, (0,), far_counts, 2)
        o2a, o2b = over_cell(o2a, 1), over_cell(o2b, 1)
        m3a, m3b = m3a + o3a, m3b + o3b
        o1, m1 = sums_of(after(near_at, m3b, m2a), near, (1,), near_counts, 1)
        o1 = over_cell(o1, 1)
        m3a, m3b = over_cell(m3a, 2), over_cell(m3b, 2)
        m2a, m2b = m2a + o2a + m3a, m2b + o2b + m3b
        o0, m0 = sums_of(after(near_at, m2b, m1), near, (0,), near_counts, 1)
        m2a, m2b = over_cell(m2a, 4), over_cell(m2b, 4)
        m1 = over_cell(m1 + o1, 2)
        m0 = m0 + over_cell(o0, 1)
        own_v = stepped(own_v, m0 + m1 + jnp.concatenate([m2a, m2b], axis=0))
        if iteration + 1 < ITERS:
            near, far = gather_loadings(own_v)

    new_u = jnp.where(x == 0, own_u[:, :64], own_u[:, 64:])
    new_v = jnp.concatenate([own_v[:, :64], own_v[:, 64:]], axis=0)
    return new_u, new_v


def predict(factor_rows, loading_rows, cell_part, gene_part, count_part):
    linear = jnp.dot(
        factor_rows,
        loading_rows.T,
        preferred_element_type=jnp.float32,
        precision=lax.Precision.HIGHEST,
    )
    linear = linear + cell_part[:, None] + gene_part[None, :]
    means = jnp.exp(linear)
    excess = means - count_part.astype(jnp.float32)
    return (means, excess)


def plain_sweeps(counts, factors, loadings, cell_offset, gene_offset):
    rank = factors.shape[1]
    precise = dict(preferred_element_type=F32, precision=lax.Precision.HIGHEST)
    contract = (((0,), (0,)), ((), ()))
    own_u, own_v = factors, loadings
    u = lax.all_gather(own_u, "gene", axis=0, tiled=True)
    v = lax.all_gather(own_v, "cell", axis=0, tiled=True)
    for iteration in range(ITERS):
        means, excess = predict(u, v, cell_offset, gene_offset, counts)
        grad = jnp.dot(excess, v, **precise)
        curv = jnp.dot(means, v * v, **precise)
        shares = lax.psum_scatter(
            jnp.concatenate([grad, curv], axis=1), "gene", scatter_dimension=0, tiled=True
        )
        own_u = own_u - bounded(shares[:, :rank] / (shares[:, rank:] + epsilon))
        u = lax.all_gather(own_u, "gene", axis=0, tiled=True)
        means, excess = predict(u, v, cell_offset, gene_offset, counts)
        grad = lax.dot_general(excess, u, contract, **precise)
        curv = lax.dot_general(means, u * u, contract, **precise)
        shares = lax.psum_scatter(
            jnp.concatenate([grad, curv], axis=1), "cell", scatter_dimension=0, tiled=True
        )
        own_v = own_v - bounded(shares[:, :rank] / (shares[:, rank:] + epsilon))
        if iteration + 1 < ITERS:
            v = lax.all_gather(own_v, "cell", axis=0, tiled=True)
    return own_u, own_v


def solution(mesh):
    n_cell, n_gene = mesh.shape["cell"], mesh.shape["gene"]
    in_specs = (
        P("cell", "gene"),
        P(("cell", "gene"), None),
        P(("gene", "cell"), None),
        P("cell"),
        P("gene"),
    )
    out_specs = (P(("cell", "gene"), None), P(("gene", "cell"), None))
    per_device = plain_sweeps
    if (n_cell, n_gene) == (8, 4):
        per_device = functools.partial(overlapped, n_cell=n_cell, n_gene=n_gene)
    return jax.shard_map(
        per_device, mesh=mesh, in_specs=in_specs, out_specs=out_specs, check_vma=False
    )
```

```python
import functools

import jax
import jax.numpy as jnp
from jax import lax
from jax.experimental import pallas as pl
from jax.experimental.pallas import tpu as pltpu
from jax.sharding import PartitionSpec as P

ITERS = 2
LOG2E = 1.4426950408889634
BF = jnp.bfloat16
F32 = jnp.float32
NT = (((1,), (1,)), ((), ()))

epsilon = 1e-06
step_cap = 0.25


def bounded(ratio):
    return step_cap * jnp.tanh(ratio / step_cap)


def params(megabytes=14):
    return pltpu.CompilerParams(vmem_limit_bytes=megabytes * 2**20)


def pack(rows):
    half = rows.shape[0] // 2
    return jnp.concatenate([rows[:half], rows[half:]], axis=1)


def left_lanes(shape):
    return lax.broadcasted_iota(jnp.int32, shape, 1) < 64


def doubled(packed):
    turned = pltpu.roll(packed, 64, 1)
    left = left_lanes(packed.shape)
    return jnp.concatenate(
        [jnp.where(left, packed, turned), jnp.where(left, turned, packed)], axis=0
    )


def parts(x):
    hi = x.astype(BF).astype(F32)
    return hi, x - hi


def pick(left, a, b):
    return jnp.where(left, a, b).astype(BF)


def queries(x, offset):
    left = left_lanes(x.shape)
    hi, lo = parts(x * LOG2E)
    return jnp.concatenate([pick(left, hi, lo), pick(left, hi, offset.astype(F32))], axis=1)


def keys(x, offset):
    left = left_lanes(x.shape)
    hi, lo = parts(x)
    return jnp.concatenate([hi.astype(BF), pick(left, lo, offset.astype(F32))], axis=1)


def weights(x):
    left = left_lanes(x.shape)
    hi, lo = parts(x)
    square_hi, square_lo = parts(x * x)
    both = jnp.concatenate([pick(left, hi, square_hi), pick(left, lo, square_lo)], axis=1)
    grad = jnp.concatenate([pick(left, -hi, 0.0), pick(left, -lo, 0.0)], axis=1)
    return both, grad


def sums(query, key, weight, count, count_weight):
    linear = lax.dot_general(query, key, NT, preferred_element_type=F32)
    means = jnp.exp2(linear)
    hi = means.astype(BF)
    lo = (means - hi.astype(F32)).astype(BF)
    total = jnp.dot(
        jnp.concatenate([hi, lo, count], axis=1),
        jnp.concatenate([weight, weight, count_weight], axis=0),
        preferred_element_type=F32,
    )
    return total[:, :128] + total[:, 128:]


def columns_kernel(is_cell, offset_ref, out_ref):
    hi, rest = parts(offset_ref[...] * LOG2E)
    mid, low = parts(rest)
    shape = (128, offset_ref.shape[1])
    row = lax.broadcasted_iota(jnp.int32, shape, 0)
    first, ones = (64, 67) if is_cell else (67, 64)
    lines = jnp.where((row >= ones) & (row < ones + 3), 1.0, 0.0)
    for at, part in enumerate((hi, mid, low)):
        lines = jnp.where(row == first + at, part, lines)
    out_ref[...] = lines.T.astype(BF)


def columns_call(offset, is_cell):
    size = offset.shape[0]
    return pl.pallas_call(
        functools.partial(columns_kernel, is_cell),
        out_shape=jax.ShapeDtypeStruct((size, 128), BF),
        compiler_params=params(),
        cost_estimate=work(0, 0),
    )(offset.reshape(1, size))


def count_kernel(tile, where, count_ref, plain_ref, turned_ref):
    at = pl.ds(pl.multiple_of(pl.program_id(0) * tile, tile), tile)
    x = count_ref[...].astype(F32).astype(BF)
    plain_ref[:, at] = x
    turned_ref[at, :] = x.T


def count_call(where, counts, blocks=2, tile=512):
    cells, genes = counts.shape
    genes = genes // blocks
    steps = genes // tile
    return pl.pallas_call(
        functools.partial(count_kernel, tile),
        grid_spec=pltpu.PrefetchScalarGridSpec(
            num_scalar_prefetch=1,
            grid=(steps,),
            in_specs=[pl.BlockSpec((cells, tile), lambda j, w: (0, w[0] * steps + j))],
            out_specs=[pl.BlockSpec(memory_space=pltpu.VMEM)] * 2,
        ),
        out_shape=[
            jax.ShapeDtypeStruct((cells, genes), BF),
            jax.ShapeDtypeStruct((genes, cells), BF),
        ],
        compiler_params=params(42),
        cost_estimate=pl.CostEstimate(flops=0, bytes_accessed=cells * genes * 6, transcendentals=0),
    )(where, counts)


def work(cells, genes):
    return pl.CostEstimate(
        flops=2 * cells * genes * 256 * 4,
        bytes_accessed=2 * cells * genes,
        transcendentals=cells * genes,
    )


def factor_rows(core, mine_ref, other_ref):
    mine, other = mine_ref[...], other_ref[...]
    first = jnp.where(core == 0, mine, other)
    second = jnp.where(core == 0, other, mine)
    return doubled(jnp.concatenate([first, second], axis=0))


def chunk_base(where, slot, place, size):
    at = (jnp.bitwise_xor(where[1], slot) * 2 + place) * size
    return pl.multiple_of(at, size)


def factor_kernel(last, where, mine_u, other_u, cell_ref, v0, w0, v1, w1, gene_ref, count_ref, turned_ref, *rest):
    y, core = where[2], where[3]
    if last:
        sum_ref, keep_ref, send_ref, query_ref = rest
    else:
        out_ref, query_ref = rest
    query_ref[...] = queries(factor_rows(core, mine_u, other_u), cell_ref[...])
    size = v0.shape[0] * 2
    chunks = []
    for slot, refs in enumerate(((v0, w0), (v1, w1))):
        for place, ref in zip((y, 1 - y), refs):
            base = chunk_base(where, slot, place, size)
            v = doubled(ref[...])
            at = pl.ds(base, size)
            chunks.append((at, keys(v, gene_ref[at, :]), *weights(v)))
    rows = mine_u.shape[0]

    def partial_sums(row):
        span = pl.ds(row, rows)
        query = query_ref[span, :]
        total = sum_ref[span, :] if last else None
        for at, key, weight, count_weight in chunks:
            part = sums(query, key, weight, count_ref[span, at], count_weight)
            total = part if total is None else total + part
        return total

    for side in range(2):
        if last:
            for target, place in ((send_ref, 1 - core), (keep_ref, core)):
                row = pl.multiple_of(side * 2 * rows + place * rows, rows)
                target[side * rows : (side + 1) * rows, :] = partial_sums(row)
        else:
            for row in (side * 2 * rows, side * 2 * rows + rows):
                out_ref[row : row + rows, :] = partial_sums(row)


def block_specs(arrays):
    return [pl.BlockSpec(a.shape, lambda j, w: (0, 0)) for a in arrays]


def factor_call(where, u, cell_columns, v, gene_columns, counts, total=None):
    cells = counts[0].shape[0]
    tile = 8 * v[0].shape[0]
    last = total is not None
    whole = [*u, cell_columns, *v]
    extra = [total] if last else []
    shapes = [(cells // 2, 128)] * 2 if last else [(cells, 128)]
    return pl.pallas_call(
        functools.partial(factor_kernel, last),
        grid_spec=pltpu.PrefetchScalarGridSpec(
            num_scalar_prefetch=1,
            grid=(1,),
            in_specs=block_specs(whole)
            + [
                pl.BlockSpec((tile, 128), lambda j, w: (w[0], 0)),
                pl.BlockSpec(memory_space=pltpu.VMEM),
                pl.BlockSpec(memory_space=pl.ANY),
            ]
            + block_specs(extra),
            out_specs=[pl.BlockSpec(shape, lambda j, w: (0, 0)) for shape in shapes],
            scratch_shapes=[pltpu.VMEM((cells, 256), BF)],
        ),
        out_shape=[jax.ShapeDtypeStruct(shape, F32) for shape in shapes],
        compiler_params=params(),
        cost_estimate=work(cells, tile),
    )(where, *whole, gene_columns, *counts, *extra)


def opening_kernel(
    where, mine_u, other_u, cell_ref, v0, w0, v1, w1, gene_ref, count_ref, turned_ref, raw_ref,
    out_ref, plain_out, turned_out, query_ref, key_ref, weight_ref, grad_ref,
):
    y, core = where[2], where[3]
    step = pl.program_id(0)
    size = v0.shape[0] * 2
    rows = mine_u.shape[0]
    places = [(slot, place) for slot in range(2) for place in (y, 1 - y)]

    @pl.when(step == 0)
    def _():
        query_ref[...] = queries(factor_rows(core, mine_u, other_u), cell_ref[...])
        for i, (at, ref) in enumerate(zip(places, (v0, w0, v1, w1))):
            v = doubled(ref[...])
            key_ref[i] = keys(v, gene_ref[pl.ds(chunk_base(where, *at, size), size), :])
            weight_ref[i], grad_ref[i] = weights(v)

    span = pl.ds(pl.multiple_of(step * rows, rows), rows)
    total = None
    for i, at in enumerate(places):
        count = count_ref[span, pl.ds(chunk_base(where, *at, size), size)]
        part = sums(query_ref[span, :], key_ref[i], weight_ref[i], count, grad_ref[i])
        total = part if total is None else total + part
    out_ref[span, :] = total
    columns = pl.ds(pl.multiple_of(step * size, size), size)
    x = raw_ref[...].astype(F32).astype(BF)
    plain_out[:, columns] = x
    turned_out[columns, :] = x.T


def opening_call(where, u, cell_columns, v, gene_columns, counts, raw):
    cells = raw.shape[0]
    size = 2 * v[0].shape[0]
    tile = 4 * size
    whole = [*u, cell_columns, *v]
    out_shape = [
        jax.ShapeDtypeStruct((cells, 128), F32),
        jax.ShapeDtypeStruct((cells, tile), BF),
        jax.ShapeDtypeStruct((tile, cells), BF),
    ]
    return pl.pallas_call(
        opening_kernel,
        grid_spec=pltpu.PrefetchScalarGridSpec(
            num_scalar_prefetch=1,
            grid=(4,),
            in_specs=block_specs(whole)
            + [
                pl.BlockSpec((tile, 128), lambda j, w: (w[0], 0)),
                pl.BlockSpec(memory_space=pltpu.VMEM),
                pl.BlockSpec(memory_space=pl.ANY),
                pl.BlockSpec((cells, size), lambda j, w: (0, (1 - w[0]) * 4 + j)),
            ],
            out_specs=[pl.BlockSpec((cells, 128), lambda j, w: (0, 0))]
            + [pl.BlockSpec(memory_space=pltpu.VMEM)] * 2,
            scratch_shapes=[pltpu.VMEM((cells, 256), BF)] + [pltpu.VMEM((4, size, 256), BF)] * 3,
        ),
        out_shape=out_shape,
        compiler_params=params(34),
        cost_estimate=work(cells, tile),
    )(where, *whole, gene_columns, *counts, raw)


def loading_kernel(pieces, slots, where, mine_u, other_u, cell_ref, *rest):
    y, core = where[2], where[3]
    count = 2 * len(slots)
    v, (gene_ref, turned_ref), outs = rest[:count], rest[count:][:2], iter(rest[count + 2 :])
    u = factor_rows(core, mine_u, other_u)
    key = keys(u, cell_ref[...])
    weight, count_weight = weights(u)
    size = v[0].shape[0] * 2
    rows = size // 2
    for i, slot in enumerate(slots):
        for place, ref in ((1 - y, v[2 * i + 1]), (y, v[2 * i])):
            base = chunk_base(where, slot, place, size)
            query = queries(doubled(ref[...]), gene_ref[pl.ds(base, size), :])
            for half in range(2):
                if half == 0 or pieces == 2:
                    target = next(outs)
                row = half * rows if pieces == 1 else 0
                part = turned_ref[pl.ds(pl.multiple_of(base + half * rows, rows), rows), :]
                span = slice(half * rows, (half + 1) * rows)
                target[row : row + rows, :] = sums(query[span], key, weight, part, count_weight)


def loading_call(where, u, cell_columns, v, slots, gene_columns, turned, pieces):
    cells = turned.shape[1]
    half = v[0].shape[0]
    v = [part for slot in slots for part in v[2 * slot : 2 * slot + 2]]
    whole = [*u, cell_columns, *v]
    shapes = [(2 * half // pieces, 128)] * (2 * len(slots) * pieces)
    return pl.pallas_call(
        functools.partial(loading_kernel, pieces, slots),
        grid_spec=pltpu.PrefetchScalarGridSpec(
            num_scalar_prefetch=1,
            grid=(1,),
            in_specs=block_specs(whole)
            + [
                pl.BlockSpec((8 * half, 128), lambda j, w: (w[0], 0)),
                pl.BlockSpec(memory_space=pltpu.VMEM),
            ],
            out_specs=[pl.BlockSpec(shape, lambda j, w: (0, 0)) for shape in shapes],
        ),
        out_shape=[jax.ShapeDtypeStruct(shape, F32) for shape in shapes],
        compiler_params=params(),
        cost_estimate=work(cells, 4 * half * len(slots)),
    )(where, *whole, gene_columns, turned)


def stepped(packed, total):
    half = packed.shape[0]
    step = bounded(total[:, :64] / (total[:, 64:] + epsilon))
    return packed - jnp.concatenate([step[:half], step[half:]], axis=1)


def swap(x, axis, size, mask):
    return lax.ppermute(x, axis, [(i, i ^ mask) for i in range(size)])


def after(value, *others):
    return lax.optimization_barrier((value, *others))[0]


def overlapped(counts, factors, loadings, cell_offset, gene_offset, n_cell, n_gene):
    cell = lax.axis_index("cell")
    gene = lax.axis_index("gene")
    core, x = gene % 2, gene // 2
    y, z = cell % 2, cell // 2

    def over_cell(value, mask):
        return swap(value, "cell", n_cell, mask)

    def over_gene(value, mask):
        return swap(value, "gene", n_gene, mask)

    def gather_loadings(own):
        mine = [own] + [over_cell(own, 2 * s) for s in range(1, 4)]
        other = [over_cell(m, 1) for m in mine]
        return (mine[0], other[0], mine[1], other[1]), (mine[2], other[2], mine[3], other[3])

    own_v = pack(loadings)
    theirs = over_gene(factors, 2)
    own_u = jnp.where(
        x == 0,
        jnp.concatenate([factors, theirs], axis=1),
        jnp.concatenate([theirs, factors], axis=1),
    )
    u = (own_u, over_gene(own_u, 1))
    near, far = gather_loadings(own_v)
    cell_columns = columns_call(cell_offset, True)
    gene_columns = columns_call(gene_offset, False)
    near_at = jnp.stack([z // 2, z % 2, y, core])
    far_at = jnp.stack([(z // 2) ^ 1, z % 2, y, core])
    near_counts = far_counts = None

    for iteration in range(ITERS):
        if iteration == 0:
            near_counts = count_call(near_at, counts)
        if iteration == 0:
            total, *far_counts = opening_call(
                near_at, u, cell_columns, near, gene_columns, near_counts, counts
            )
        else:
            (total,) = factor_call(near_at, u, cell_columns, near, gene_columns, near_counts)
        keep, send = factor_call(far_at, u, cell_columns, far, gene_columns, far_counts, total)
        keep = keep + over_gene(send, 1)
        keep = keep + over_gene(keep, 2)
        own_u = stepped(own_u, keep)
        u = (own_u, over_gene(own_u, 1))

        def sums_of(at, v, slots, block, pieces):
            return loading_call(at, u, cell_columns, v, slots, gene_columns, block[1], pieces)

        o3a, o3b, m3a, m3b = sums_of(far_at, far, (1,), far_counts, 2)
        o3a, o3b = over_cell(o3a, 1), over_cell(o3b, 1)
        o2a, o2b, m2a, m2b = sums_of(after(far_at, m3a), far, (0,), far_counts, 2)
        o2a, o2b = over_cell(o2a, 1), over_cell(o2b, 1)
        m3a, m3b = m3a + o3a, m3b + o3b
        o1, m1 = sums_of(after(near_at, m3b, m2a), near, (1,), near_counts, 1)
        o1 = over_cell(o1, 1)
        m3a, m3b = over_cell(m3a, 2), over_cell(m3b, 2)
        m2a, m2b = m2a + o2a + m3a, m2b + o2b + m3b
        o0, m0 = sums_of(after(near_at, m2b), near, (0,), near_counts, 1)
        m2a, m2b = over_cell(m2a, 4), over_cell(m2b, 4)
        m1 = over_cell(m1 + o1, 2)
        m0 = m0 + over_cell(o0, 1)
        own_v = stepped(own_v, m0 + m1 + jnp.concatenate([m2a, m2b], axis=0))
        if iteration + 1 < ITERS:
            near, far = gather_loadings(own_v)

    new_u = jnp.where(x == 0, own_u[:, :64], own_u[:, 64:])
    new_v = jnp.concatenate([own_v[:, :64], own_v[:, 64:]], axis=0)
    return new_u, new_v


def predict(factor_rows, loading_rows, cell_part, gene_part, count_part):
    linear = jnp.dot(
        factor_rows,
        loading_rows.T,
        preferred_element_type=jnp.float32,
        precision=lax.Precision.HIGHEST,
    )
    linear = linear + cell_part[:, None] + gene_part[None, :]
    means = jnp.exp(linear)
    excess = means - count_part.astype(jnp.float32)
    return (means, excess)


def plain_sweeps(counts, factors, loadings, cell_offset, gene_offset):
    rank = factors.shape[1]
    precise = dict(preferred_element_type=F32, precision=lax.Precision.HIGHEST)
    contract = (((0,), (0,)), ((), ()))
    own_u, own_v = factors, loadings
    u = lax.all_gather(own_u, "gene", axis=0, tiled=True)
    v = lax.all_gather(own_v, "cell", axis=0, tiled=True)
    for iteration in range(ITERS):
        means, excess = predict(u, v, cell_offset, gene_offset, counts)
        grad = jnp.dot(excess, v, **precise)
        curv = jnp.dot(means, v * v, **precise)
        shares = lax.psum_scatter(
            jnp.concatenate([grad, curv], axis=1), "gene", scatter_dimension=0, tiled=True
        )
        own_u = own_u - bounded(shares[:, :rank] / (shares[:, rank:] + epsilon))
        u = lax.all_gather(own_u, "gene", axis=0, tiled=True)
        means, excess = predict(u, v, cell_offset, gene_offset, counts)
        grad = lax.dot_general(excess, u, contract, **precise)
        curv = lax.dot_general(means, u * u, contract, **precise)
        shares = lax.psum_scatter(
            jnp.concatenate([grad, curv], axis=1), "cell", scatter_dimension=0, tiled=True
        )
        own_v = own_v - bounded(shares[:, :rank] / (shares[:, rank:] + epsilon))
        if iteration + 1 < ITERS:
            v = lax.all_gather(own_v, "cell", axis=0, tiled=True)
    return own_u, own_v


def solution(mesh):
    n_cell, n_gene = mesh.shape["cell"], mesh.shape["gene"]
    in_specs = (
        P("cell", "gene"),
        P(("cell", "gene"), None),
        P(("gene", "cell"), None),
        P("cell"),
        P("gene"),
    )
    out_specs = (P(("cell", "gene"), None), P(("gene", "cell"), None))
    per_device = plain_sweeps
    if (n_cell, n_gene) == (8, 4):
        per_device = functools.partial(overlapped, n_cell=n_cell, n_gene=n_gene)
    return jax.shard_map(
        per_device, mesh=mesh, in_specs=in_specs, out_specs=out_specs, check_vma=False
    )
```
